1024 devices in a mesh: loop: 32 (over z_lo, x, core), grp: 32 (over z_hi, y).
Axes of the slice: x: 8, y: 8, z: 8 (z_hi: 4, z_lo: 2; z = z_hi * 2 + z_lo), core: 2. Of those that a mesh axis runs over, the one named last changes fastest.
Arguments:
- picture_features: float32 [262144, 1152], P(('loop', 'grp')), may hold values from -1.0298836 to 1.0298836
- caption_features_per_holder: float32 [131072, 1152], P(('loop', 'grp')), may hold values from -1.0298836 to 1.0298836
- dispatched_entries: int32 [32, 32, 32, 6], P('loop', 'grp'), may hold values from 0 to 127, as said below
- sent_tally: int32 [32, 32, 32], P('loop'), may hold values from 2 to 6, as said below
- positive_caption_position: int32 [262144], P(('loop', 'grp')), may hold values from 0 to 131071, as said below
- score_scale_factor: float32 [1], replicated, may hold values from 1 to 3
- score_shift_term: float32 [1], replicated, may hold values from -4 to -1
Outputs:
- image_grad: float32 [262144, 1152], P(('loop', 'grp'))
- text_grad: float32 [131072, 1152], P(('loop', 'grp'))
The draws below stay inside these ranges and needn't reach their ends.
Inputs may be any that keep to these rules, and one draw needn't show every extreme that they name: sent_tally[l, g', g] rows go from owner (l, g') to device (l, g); every row and every column of sent_tally[l] sums to 128, and every row and every column holds an entry equal to 6. For c < sent_tally[l, g', g], dispatched_entries[l, g', g, c] names one of owner (l, g')'s owned rows; over all g and such c, each owned row is named exactly once. Later slots hold arbitrary row numbers. `positive_caption_position`: the positive text row of an image row of block (l, g) lies in text block (l - k mod 32, g) for some k < 4.
All inputs are finite; a program needn't handle non-finite values.
Results may differ from the reference program's by a relative error of at most 0.0049.
Values may be sent and summed in bfloat16 or wider, within the bound.
No kernel may reach another device: no remote copies, remote signals or barrier semaphores. Data moves between devices by JAX's collectives and lax.ppermute only.
A program may use at most 32 MiB of HBM per device.

```python
import jax
import jax.numpy as jnp
from jax import lax

D = 1152
IMG_ROWS = 256
TEXT_ROWS = 128
STOPS = 4
LOOPS = 32
OWNERS = 32
SHARE = 4
CAP = 6


def count_table(key):

    def single_iteration(single):
        key_list = jax.random.split(single, 3)
        shifts = jax.random.permutation(key_list[0], OWNERS)[:4]
        row_order = jax.random.permutation(key_list[1], OWNERS)
        column_order = jax.random.permutation(key_list[2], OWNERS)
        offset = (column_order[None, :] - row_order[:, None]) % OWNERS
        half_share = SHARE // 2
        quarter = SHARE // 4
        counts_table = SHARE + half_share * ((offset == shifts[0]).astype(jnp.int32) - (offset == shifts[1]).astype(jnp.int32))
        counts_table = counts_table + quarter * ((offset == shifts[2]).astype(jnp.int32) - (offset == shifts[3]).astype(jnp.int32))
        return counts_table.astype(jnp.int32)
    return jax.vmap(single_iteration)(jax.random.split(key, LOOPS))


def draw_sent_tally(key, part):
    return count_table(key)


def draw_dispatched_entries(key, part):
    counts_table = count_table(key)
    key = jax.random.fold_in(key, 7)
    orders = jax.vmap(lambda single: jax.random.permutation(single, TEXT_ROWS))(jax.random.split(key, LOOPS * OWNERS))
    orders = orders.reshape(LOOPS, OWNERS, 1, TEXT_ROWS).astype(jnp.int32)
    offsets = jnp.cumsum(counts_table, axis=2) - counts_table
    picked = (offsets[..., None] + jnp.arange(CAP, dtype=jnp.int32)) % TEXT_ROWS
    spread = jnp.broadcast_to(orders, (LOOPS, OWNERS, OWNERS, TEXT_ROWS))
    return jnp.take_along_axis(spread, picked, axis=3).astype(jnp.int32)


def draw_positive_caption_position(key, part):
    key = jax.random.fold_in(key, 11)
    key_stop, key_row = jax.random.split(key)
    row_total = LOOPS * OWNERS * IMG_ROWS
    stop_draw = jax.random.randint(key_stop, (row_total,), 0, STOPS)
    picked = jax.random.randint(key_row, (row_total,), 0, TEXT_ROWS)
    row_ids = jnp.arange(row_total, dtype=jnp.int32)
    loop_ids = row_ids // (OWNERS * IMG_ROWS)
    group_ids = row_ids // IMG_ROWS % OWNERS
    stop_draw = stop_draw.at[0].set(0).at[-1].set(0)
    picked = picked.at[0].set(0).at[-1].set(TEXT_ROWS - 1)
    return (((loop_ids - stop_draw) % LOOPS * OWNERS + group_ids) * TEXT_ROWS + picked).astype(jnp.int32)


def steps_of(own_key, dims, cuts, least, top_value):
    factor_of = 1.0
    for dim, blocks in cuts:
        heights = jax.random.uniform(jax.random.fold_in(jax.random.fold_in(own_key, 6), dim), (blocks,), jnp.float32, least / len(cuts), top_value / len(cuts))
        factor_of = factor_of * jnp.repeat(jnp.exp(heights), dims[dim] // blocks).reshape((-1,) + (1,) * (len(dims) - 1 - dim))
    return factor_of


def scatter_about(own_key, dims, width, most, cuts=(), held_as=jnp.bfloat16):
    entries = width * jax.random.normal(own_key, dims, jnp.float32)
    if cuts:
        entries = entries * steps_of(own_key, dims, cuts, -0.22, 0.18)
    return jnp.clip(entries, -most, most).astype(held_as)


def setup_inputs(seed: int = 0) -> dict:
    key_of = jax.random.split(jax.random.key(seed), 8)
    return {
        "picture_features": scatter_about(key_of[0], (LOOPS * OWNERS * IMG_ROWS, D), (D ** -0.25), 1.0298836, ((0, 1024),), jnp.float32),
        "caption_features_per_holder": scatter_about(key_of[1], (LOOPS * OWNERS * TEXT_ROWS, D), (D ** -0.25), 1.0298836, ((0, 1024),), jnp.float32),
        "dispatched_entries": draw_dispatched_entries(jax.random.fold_in(key_of[7], 71), 0),
        "sent_tally": draw_sent_tally(jax.random.fold_in(key_of[7], 71), 0),
        "positive_caption_position": draw_positive_caption_position(jax.random.fold_in(key_of[7], 71), 0),
        "score_scale_factor": jnp.clip(jax.random.uniform(key_of[5], (1,), jnp.float32, 1.0, 3.0), 1.0, 3.0),
        "score_shift_term": jnp.clip(jax.random.uniform(key_of[6], (1,), jnp.float32, -4.0, -1.0), -4.0, -1.0),
    }


def slopes_for(image_part, text_part, positives, first_id, score_scaling_factor, logit_offset_bias):
    scores = lax.dot_general(image_part, text_part, (((1,), (1,)), ((), ())), preferred_element_type=jnp.float32)
    logits = score_scaling_factor * scores + logit_offset_bias
    columns = first_id + jnp.arange(text_part.shape[0], dtype=jnp.int32)
    signed = jnp.where(positives[:, None] == columns[None, :], 1.0, -1.0).astype(jnp.float32)
    return (-score_scaling_factor * signed * jax.nn.sigmoid(-signed * logits)).astype(jnp.bfloat16)


def placement_rows(dispatched_entries, sent_tally):
    end_marks = jnp.transpose(jnp.cumsum(sent_tally, axis=1), (0, 2, 1))
    start_marks = end_marks - jnp.transpose(sent_tally, (0, 2, 1))
    places = jnp.arange(TEXT_ROWS, dtype=jnp.int32)
    source = jnp.sum((end_marks[:, :, None, :] <= places[None, None, :, None]).astype(jnp.int32), axis=3)
    within = places[None, None, :] - jnp.take_along_axis(start_marks, source, axis=2)
    loop_ids = jnp.arange(LOOPS, dtype=jnp.int32)[:, None, None]
    group_ids = jnp.arange(OWNERS, dtype=jnp.int32)[None, :, None]
    owned_row = dispatched_entries[loop_ids, source, group_ids, within]
    return ((loop_ids * OWNERS + source) * TEXT_ROWS + owned_row).reshape(-1).astype(jnp.int32)


def reference(picture_features, caption_features_per_holder, dispatched_entries, sent_tally, positive_caption_position, score_scale_factor, score_shift_term):
    features = picture_features.shape[1]
    score_scaling_factor = score_scale_factor[0]
    logit_offset_bias = score_shift_term[0]
    image_low = picture_features.astype(jnp.bfloat16).reshape(LOOPS, OWNERS, IMG_ROWS, features)
    owner_rows = placement_rows(dispatched_entries, sent_tally)
    blocks = caption_features_per_holder.astype(jnp.bfloat16)[owner_rows].reshape(LOOPS, OWNERS, TEXT_ROWS, features)
    positives = positive_caption_position.reshape(LOOPS, OWNERS, IMG_ROWS)

    def image_block(block_index):
        loop_at = block_index // OWNERS
        group_at = block_index % OWNERS
        image_part = image_low[loop_at, group_at]
        gathered = jnp.zeros((IMG_ROWS, features), jnp.float32)
        for stop_index in range(STOPS):
            anchor = (loop_at - stop_index) % LOOPS
            text_part = blocks[anchor, group_at]
            slopes = slopes_for(image_part, text_part, positives[loop_at, group_at],
                                (anchor * OWNERS + group_at) * TEXT_ROWS, score_scaling_factor, logit_offset_bias)
            gathered = gathered + jnp.dot(slopes, text_part, preferred_element_type=jnp.float32)
        return gathered

    def text_block(block_index):
        loop_at = block_index // OWNERS
        group_at = block_index % OWNERS
        text_part = blocks[loop_at, group_at]
        summed = jnp.zeros((TEXT_ROWS, features), jnp.float32)
        for stop_index in range(STOPS):
            source_loop = (loop_at + stop_index) % LOOPS
            image_part = image_low[source_loop, group_at]
            slopes = slopes_for(image_part, text_part, positives[source_loop, group_at],
                                (loop_at * OWNERS + group_at) * TEXT_ROWS, score_scaling_factor, logit_offset_bias)
            summed = summed + lax.dot_general(slopes, image_part, (((0,), (0,)), ((), ())),
                                              preferred_element_type=jnp.float32)
        return summed

    indices = jnp.arange(LOOPS * OWNERS, dtype=jnp.int32)
    image_grad = lax.map(image_block, indices).reshape(-1, features)
    block_grad = lax.map(text_block, indices).reshape(-1, features)
    text_grad = jnp.zeros_like(block_grad).at[owner_rows].set(block_grad)
    return image_grad, text_grad
```

```python
import jax
import jax.numpy as jnp
from jax import lax
from jax.experimental import pallas as pl
from jax.experimental.pallas import tpu as pltpu
from jax.sharding import PartitionSpec as P

STOPS = 4
LANES = 128
AUX_ROWS = 16
BF16 = jnp.bfloat16
F32 = jnp.float32


def passed_along(value, axis, steps):
    count = lax.axis_size(axis)
    pairs = [(source, (source + steps) % count) for source in range(count)]
    return lax.ppermute(value, axis, pairs)


def iota(shape, dim):
    return lax.broadcasted_iota(jnp.int32, shape, dim)


def rows_to_chunks(rows, staging, chunks_ref):
    peers, chunk_rows, _ = chunks_ref.shape
    pitch = staging.shape[0] // peers
    tiles = rows.shape[1] // LANES
    for slot in range(rows.shape[0] // peers):
        for tile in range(tiles):
            staging[pl.ds(slot * tiles + tile, peers, stride=pitch), :] = rows[
                slot * peers : (slot + 1) * peers, tile * LANES : (tile + 1) * LANES
            ]
    for peer in range(peers):
        chunks_ref[peer] = staging[peer * pitch : peer * pitch + chunk_rows, :].astype(chunks_ref.dtype)


def chunks_to_rows(chunks_ref, staging, rows_ref):
    peers, chunk_rows, _ = chunks_ref.shape
    pitch = staging.shape[0] // peers
    tiles = rows_ref.shape[1] // LANES
    for peer in range(peers):
        staging[peer * pitch : peer * pitch + chunk_rows, :] = chunks_ref[peer].astype(F32)
    for slot in range(rows_ref.shape[0] // peers):
        for tile in range(tiles):
            rows_ref[slot * peers : (slot + 1) * peers, tile * LANES : (tile + 1) * LANES] = staging[
                pl.ds(slot * tiles + tile, peers, stride=pitch), :
            ].astype(rows_ref.dtype)


def hits(columns, width):
    return jnp.concatenate(
        [(column == iota((column.shape[0], width), 1)).astype(F32) for column in columns], axis=0
    ).astype(BF16)


def block_places(tally, group_at, slot_cap, width):
    peers = tally.shape[0]
    mine = jnp.where(iota(tally.shape, 1) == group_at, tally, 0)
    before = (iota((peers, peers), 1) < iota((peers, peers), 0)).astype(F32)
    starts = jnp.dot(before, mine.astype(F32), preferred_element_type=F32)
    incoming = jnp.sum(mine, axis=1, keepdims=True)
    first = jnp.sum(starts, axis=1, keepdims=True).astype(jnp.int32)
    return hits([jnp.where(incoming > slot, first + slot, -1) for slot in range(slot_cap)], width)


def slopes_for(text, image, places, scale, shift):
    scores = lax.dot_general(text, image, (((1,), (1,)), ((), ())), preferred_element_type=F32)
    logits = scale * scores + shift
    positive = places == iota(scores.shape, 0)
    toward = jax.nn.sigmoid(jnp.where(positive, -logits, logits))
    return (jnp.where(positive, -scale, scale) * toward).astype(BF16)


def picture_kernel(loop_count, group_count, text_rows, picture_ref, positive_ref, packet_ref):
    rows = picture_ref.shape[0]
    packet_ref[0:rows, :] = picture_ref[...].astype(BF16)
    positive = positive_ref[...]
    anchor = positive // (group_count * text_rows)
    behind = lax.rem(lax.axis_index("loop") - anchor + loop_count, loop_count)
    place = lax.rem(positive, text_rows)
    packet_ref[rows:, :] = jnp.zeros((AUX_ROWS, packet_ref.shape[1]), BF16)
    packet_ref[rows:, 0:rows] = jnp.where(behind == iota((AUX_ROWS, rows), 0), place, -1).astype(F32).astype(BF16)


def dispatch_kernel(caption_ref, listed_ref, chunks_ref, staging):
    listed = listed_ref[0, 0]
    chosen = hits([listed[:, slot : slot + 1] for slot in range(listed.shape[1])], caption_ref.shape[0])
    rows = jnp.dot(chosen, caption_ref[...].astype(BF16), preferred_element_type=F32)
    rows_to_chunks(rows, staging, chunks_ref)


def assemble_kernel(chunks_ref, tally_ref, block_ref, staging, rows_ref):
    slot_cap = rows_ref.shape[0] // chunks_ref.shape[0]
    chunks_to_rows(chunks_ref, staging, rows_ref)
    places = block_places(tally_ref[0], lax.axis_index("grp"), slot_cap, block_ref.shape[0])
    block_ref[...] = lax.dot_general(
        places, rows_ref[...], (((0,), (0,)), ((), ())), preferred_element_type=F32
    ).astype(BF16)


def text_kernel(scale_ref, shift_ref, tally_ref, block_ref, *refs):
    packets, chunks_ref, staging = refs[:STOPS], refs[STOPS], refs[STOPS + 1]
    scale, shift = scale_ref[0], shift_ref[0]
    text = block_ref[...]
    rows = packets[0].shape[0] - AUX_ROWS
    total = jnp.zeros(text.shape, F32)
    for stop, packet in enumerate(packets):
        image = packet[0:rows, :]
        places = packet[rows:, 0:rows].astype(F32)[stop : stop + 1, :].astype(jnp.int32)
        total = total + jnp.dot(slopes_for(text, image, places, scale, shift), image, preferred_element_type=F32)
    slot_cap = chunks_ref.shape[1] * LANES // text.shape[1]
    slots = block_places(tally_ref[0], lax.axis_index("grp"), slot_cap, text.shape[0])
    rows_to_chunks(jnp.dot(slots, total.astype(BF16), preferred_element_type=F32), staging, chunks_ref)


def image_kernel(scale_ref, shift_ref, packet_ref, *refs):
    blocks, grad_ref = refs[:STOPS], refs[STOPS]
    scale, shift = scale_ref[0], shift_ref[0]
    rows = grad_ref.shape[0]
    image = packet_ref[0:rows, :]
    aux = packet_ref[rows:, 0:rows].astype(F32)
    slopes = [
        slopes_for(block[...], image, aux[stop : stop + 1, :].astype(jnp.int32), scale, shift)
        for stop, block in enumerate(blocks)
    ]
    width = 3 * LANES
    for start in range(0, grad_ref.shape[1], width):
        total = None
        for slope, block in zip(slopes, blocks):
            part = lax.dot_general(
                slope, block[:, start : start + width], (((0,), (0,)), ((), ())), preferred_element_type=F32
            )
            total = part if total is None else total + part
        grad_ref[:, start : start + width] = total


def return_kernel(chunks_ref, listed_ref, tally_ref, grad_ref, staging, rows_ref):
    chunks_to_rows(chunks_ref, staging, rows_ref)
    listed, tally = listed_ref[0, 0], tally_ref[0]
    peers, slot_cap = listed.shape
    mine = jnp.sum(jnp.where(iota(tally.shape, 0) == lax.axis_index("grp"), tally, 0), axis=0, keepdims=True)
    upright = iota((peers, peers), 0) == iota((peers, peers), 1)
    outgoing = jnp.sum(jnp.where(upright, mine, 0), axis=1, keepdims=True)
    owned = hits(
        [jnp.where(outgoing > slot, listed[:, slot : slot + 1], -1) for slot in range(slot_cap)], grad_ref.shape[0]
    )
    grad_ref[...] = lax.dot_general(owned, rows_ref[...], (((0,), (0,)), ((), ())), preferred_element_type=F32)


def local(
    picture_features,
    caption_features_per_holder,
    dispatched_entries,
    sent_tally,
    positive_caption_position,
    score_scale_factor,
    score_shift_term,
):
    group_count = lax.axis_size("grp")
    loop_count = lax.axis_size("loop")
    image_rows, features = picture_features.shape
    text_rows = caption_features_per_holder.shape[0]
    slot_cap = dispatched_entries.shape[3]
    chunk_rows = slot_cap * features // LANES
    pitch = -(-chunk_rows // 8) * 8

    whole = pl.BlockSpec(memory_space=pltpu.VMEM)
    scalar = pl.BlockSpec(memory_space=pltpu.SMEM)
    params = pltpu.CompilerParams(vmem_limit_bytes=48 * 1024 * 1024)
    staging = pltpu.VMEM((group_count * pitch, LANES), F32)
    slot_rows = pltpu.VMEM((group_count * slot_cap, features), BF16)
    chunks = jax.ShapeDtypeStruct((group_count, chunk_rows, LANES), BF16)

    def call(kernel, in_specs, out_shape, scratch=()):
        return pl.pallas_call(
            kernel,
            out_shape=out_shape,
            in_specs=in_specs,
            out_specs=whole,
            scratch_shapes=list(scratch),
            compiler_params=params,
        )

    def picture_body(*refs):
        picture_kernel(loop_count, group_count, text_rows, *refs)

    packet = call(
        picture_body, [whole] * 2, jax.ShapeDtypeStruct((image_rows + AUX_ROWS, features), BF16)
    )(picture_features, positive_caption_position.reshape(1, -1))
    packet_two = passed_along(packet, "loop", -2)
    packet_one = passed_along(packet, "loop", -1)
    packet_three = passed_along(packet_two, "loop", -1)

    outgoing = call(dispatch_kernel, [whole] * 2, chunks, [staging])(caption_features_per_holder, dispatched_entries)
    incoming = lax.all_to_all(outgoing, "grp", split_axis=0, concat_axis=0, tiled=True)
    block = call(
        assemble_kernel, [whole] * 2, jax.ShapeDtypeStruct((text_rows, features), BF16), [staging, slot_rows]
    )(incoming, sent_tally)

    sendback = call(text_kernel, [scalar] * 2 + [whole] * (2 + STOPS), chunks, [staging])(
        score_scale_factor, score_shift_term, sent_tally, block, packet, packet_one, packet_two, packet_three
    )
    returned = lax.all_to_all(sendback, "grp", split_axis=0, concat_axis=0, tiled=True)

    block_two = passed_along(block, "loop", 2)
    block_one = passed_along(block, "loop", 1)
    block_three = passed_along(block_two, "loop", 1)
    image_grad = call(
        image_kernel, [scalar] * 2 + [whole] * (1 + STOPS), jax.ShapeDtypeStruct((image_rows, features), F32)
    )(score_scale_factor, score_shift_term, packet, block, block_one, block_two, block_three)

    text_grad = call(
        return_kernel, [whole] * 3, jax.ShapeDtypeStruct((text_rows, features), F32), [staging, slot_rows]
    )(returned, dispatched_entries, sent_tally)
    return (image_grad, text_grad)


def solution(mesh):
    placed = (
        P(("loop", "grp"), None),
        P(("loop", "grp"), None),
        P("loop", "grp", None, None),
        P("loop", None, None),
        P(("loop", "grp")),
        P(),
        P(),
    )
    return jax.shard_map(
        local,
        mesh=mesh,
        in_specs=placed,
        out_specs=(P(("loop", "grp"), None), P(("loop", "grp"), None)),
        check_vma=False,
    )
```

```python
import jax
import jax.numpy as jnp
from jax import lax
from jax.experimental import pallas as pl
from jax.experimental.pallas import tpu as pltpu
from jax.sharding import PartitionSpec as P

STOPS = 4
LANES = 128
AUX_ROWS = 16
BF16 = jnp.bfloat16
F32 = jnp.float32


def passed_along(value, axis, steps):
    count = lax.axis_size(axis)
    pairs = [(source, (source + steps) % count) for source in range(count)]
    return lax.ppermute(value, axis, pairs)


def iota(shape, dim):
    return lax.broadcasted_iota(jnp.int32, shape, dim)


def rows_to_chunks(rows, staging, chunks_ref):
    peers, chunk_rows, _ = chunks_ref.shape
    pitch = staging.shape[0] // peers
    tiles = rows.shape[1] // LANES
    for slot in range(rows.shape[0] // peers):
        for tile in range(tiles):
            staging[pl.ds(slot * tiles + tile, peers, stride=pitch), :] = rows[
                slot * peers : (slot + 1) * peers, tile * LANES : (tile + 1) * LANES
            ]
    for peer in range(peers):
        chunks_ref[peer] = staging[peer * pitch : peer * pitch + chunk_rows, :].astype(chunks_ref.dtype)


def chunks_to_rows(chunks_ref, staging, rows_ref):
    peers, chunk_rows, _ = chunks_ref.shape
    pitch = staging.shape[0] // peers
    tiles = rows_ref.shape[1] // LANES
    for peer in range(peers):
        staging[peer * pitch : peer * pitch + chunk_rows, :] = chunks_ref[peer].astype(F32)
    for slot in range(rows_ref.shape[0] // peers):
        for tile in range(tiles):
            rows_ref[slot * peers : (slot + 1) * peers, tile * LANES : (tile + 1) * LANES] = staging[
                pl.ds(slot * tiles + tile, peers, stride=pitch), :
            ].astype(rows_ref.dtype)


def hits(columns, width):
    return jnp.concatenate(
        [(column == iota((column.shape[0], width), 1)).astype(F32) for column in columns], axis=0
    ).astype(BF16)


def upright(listed_ref):
    peers = listed_ref.shape[2]
    diagonal = iota((peers, peers), 0) == iota((peers, peers), 1)
    return [
        jnp.sum(jnp.where(diagonal, listed_ref[slot], 0), axis=1, keepdims=True) for slot in range(listed_ref.shape[0])
    ]


def block_places(tally, group_at, slot_cap, width):
    peers = tally.shape[0]
    mine = jnp.where(iota(tally.shape, 1) == group_at, tally, 0)
    before = (iota((peers, peers), 1) < iota((peers, peers), 0)).astype(F32)
    starts = jnp.dot(before, mine.astype(F32), preferred_element_type=F32)
    incoming = jnp.sum(mine, axis=1, keepdims=True)
    first = jnp.sum(starts, axis=1, keepdims=True).astype(jnp.int32)
    return hits([jnp.where(incoming > slot, first + slot, -1) for slot in range(slot_cap)], width)


def places_of(packet_ref, stop):
    rows = packet_ref.shape[0] - AUX_ROWS
    kept = packet_ref[rows:, 0:rows].astype(F32)
    return jnp.sum(jnp.where(iota(kept.shape, 0) == stop, kept, 0.0), axis=0, keepdims=True).astype(jnp.int32)


def slopes_for(text, image, places, scale, shift):
    scores = lax.dot_general(text, image, (((1,), (1,)), ((), ())), preferred_element_type=F32)
    logits = scale * scores + shift
    positive = places == iota(scores.shape, 0)
    toward = jax.nn.sigmoid(jnp.where(positive, -logits, logits))
    return (jnp.where(positive, -scale, scale) * toward).astype(BF16)


def prepare_kernel(
    loop_count,
    group_count,
    picture_hbm,
    positive_hbm,
    caption_hbm,
    listed_hbm,
    packet_ref,
    chunks_ref,
    picture_ref,
    positive_ref,
    caption_ref,
    listed_ref,
    staging,
    arrived,
):
    copies = [
        pltpu.make_async_copy(source, target, arrived.at[at])
        for at, (source, target) in enumerate(
            [
                (listed_hbm, listed_ref),
                (caption_hbm, caption_ref),
                (positive_hbm, positive_ref),
                (picture_hbm, picture_ref),
            ]
        )
    ]
    for copy in copies:
        copy.start()
    text_rows = caption_ref.shape[0]
    copies[0].wait()
    chosen = hits(upright(listed_ref), text_rows)
    copies[1].wait()
    gathered = jnp.dot(chosen, caption_ref[...].astype(BF16), preferred_element_type=F32)
    rows_to_chunks(gathered, staging, chunks_ref)
    rows = picture_ref.shape[0]
    copies[2].wait()
    positive = positive_ref[...]
    anchor = positive // (group_count * text_rows)
    behind = lax.rem(lax.axis_index("loop") - anchor + loop_count, loop_count)
    place = lax.rem(positive, text_rows)
    packet_ref[rows:, :] = jnp.zeros((AUX_ROWS, packet_ref.shape[1]), BF16)
    packet_ref[rows:, 0:rows] = jnp.where(behind == iota((AUX_ROWS, rows), 0), place, -1).astype(F32).astype(BF16)
    copies[3].wait()
    packet_ref[0:rows, :] = picture_ref[...].astype(BF16)


def relay_kernel(own_ref, arrived_ref, out_ref):
    parity = lax.rem(lax.axis_index("loop"), 2)

    @pl.when(parity == 1)
    def _():
        out_ref[...] = arrived_ref[...]

    @pl.when(parity == 0)
    def _():
        out_ref[...] = own_ref[...]


def assemble_kernel(chunks_ref, tally_ref, block_ref, staging, rows_ref):
    slot_cap = rows_ref.shape[0] // chunks_ref.shape[0]
    chunks_to_rows(chunks_ref, staging, rows_ref)
    places = block_places(tally_ref[0], lax.axis_index("grp"), slot_cap, block_ref.shape[0])
    block_ref[...] = lax.dot_general(
        places, rows_ref[...], (((0,), (0,)), ((), ())), preferred_element_type=F32
    ).astype(BF16)


def text_kernel(scale_ref, shift_ref, tally_ref, block_ref, *refs):
    packets, chunks_ref, staging = refs[:STOPS], *refs[STOPS:]
    scale, shift = scale_ref[0], shift_ref[0]
    text = block_ref[...]
    rows = packets[0].shape[0] - AUX_ROWS
    odd = lax.rem(lax.axis_index("loop"), 2)
    total = jnp.zeros(text.shape, F32)
    for stop, packet in zip((0, 2, 1 + 2 * odd, 3 - 2 * odd), packets):
        image = packet[0:rows, :]
        slopes = slopes_for(text, image, places_of(packet, stop), scale, shift)
        total = total + jnp.dot(slopes, image, preferred_element_type=F32)
    slot_cap = chunks_ref.shape[1] * LANES // text.shape[1]
    slots = block_places(tally_ref[0], lax.axis_index("grp"), slot_cap, text.shape[0])
    rows_to_chunks(jnp.dot(slots, total.astype(BF16), preferred_element_type=F32), staging, chunks_ref)


def image_kernel(scale_ref, shift_ref, packet_ref, *refs):
    blocks, grad_ref = refs[:STOPS], refs[STOPS]
    scale, shift = scale_ref[0], shift_ref[0]
    rows = grad_ref.shape[0]
    image = packet_ref[0:rows, :]
    odd = lax.rem(lax.axis_index("loop"), 2)
    slopes = [
        slopes_for(block[...], image, places_of(packet_ref, stop), scale, shift)
        for stop, block in zip((0, 2, 3 - 2 * odd, 1 + 2 * odd), blocks)
    ]
    width = 3 * LANES
    for start in range(0, grad_ref.shape[1], width):
        total = None
        for slope, block in zip(slopes, blocks):
            part = lax.dot_general(
                slope, block[:, start : start + width], (((0,), (0,)), ((), ())), preferred_element_type=F32
            )
            total = part if total is None else total + part
        grad_ref[:, start : start + width] = total


def return_kernel(chunks_ref, listed_ref, tally_ref, grad_ref, staging, rows_ref):
    chunks_to_rows(chunks_ref, staging, rows_ref)
    tally = tally_ref[0]
    peers = tally.shape[0]
    mine = jnp.sum(jnp.where(iota(tally.shape, 0) == lax.axis_index("grp"), tally, 0), axis=0, keepdims=True)
    diagonal = iota((peers, peers), 0) == iota((peers, peers), 1)
    outgoing = jnp.sum(jnp.where(diagonal, mine, 0), axis=1, keepdims=True)
    owned = hits(
        [jnp.where(outgoing > slot, rows, -1) for slot, rows in enumerate(upright(listed_ref))], grad_ref.shape[0]
    )
    grad_ref[...] = lax.dot_general(owned, rows_ref[...], (((0,), (0,)), ((), ())), preferred_element_type=F32)


def local(
    picture_features,
    caption_features_per_holder,
    dispatched_entries,
    sent_tally,
    positive_caption_position,
    score_scale_factor,
    score_shift_term,
):
    group_count = lax.axis_size("grp")
    loop_count = lax.axis_size("loop")
    image_rows, features = picture_features.shape
    text_rows = caption_features_per_holder.shape[0]
    slot_cap = dispatched_entries.shape[3]
    chunk_rows = slot_cap * features // LANES
    pitch = -(-chunk_rows // 8) * 8

    whole = pl.BlockSpec(memory_space=pltpu.VMEM)
    scalar = pl.BlockSpec(memory_space=pltpu.SMEM)
    remote = pl.BlockSpec(memory_space=pltpu.HBM)
    staging = pltpu.VMEM((group_count * pitch, LANES), F32)
    slot_rows = pltpu.VMEM((group_count * slot_cap, features), BF16)
    chunks = jax.ShapeDtypeStruct((group_count, chunk_rows, LANES), BF16)
    packet_shape = jax.ShapeDtypeStruct((image_rows + AUX_ROWS, features), BF16)
    big = pl.CostEstimate(flops=6 * STOPS * image_rows * text_rows * features, bytes_accessed=8 * image_rows * features, transcendentals=0)
    huge = pl.CostEstimate(flops=50 * 1000 * 1000 * 1000, bytes_accessed=0, transcendentals=0)
    block_shape = jax.ShapeDtypeStruct((text_rows, features), BF16)

    def in_vmem(shape):
        return pltpu.VMEM(shape.shape, shape.dtype)

    def call(kernel, in_specs, out_shape, scratch=(), name=None, cost=None, limit=24):
        return pl.pallas_call(
            kernel,
            out_shape=out_shape,
            in_specs=in_specs,
            out_specs=jax.tree.map(lambda _: whole, out_shape),
            scratch_shapes=list(scratch),
            compiler_params=pltpu.CompilerParams(vmem_limit_bytes=limit * 1024 * 1024),
            name=name,
            cost_estimate=cost,
        )

    def prepare_body(*refs):
        prepare_kernel(loop_count, group_count, *refs)

    def swapped(value):
        return lax.ppermute(value, "loop", [(source, source ^ 1) for source in range(loop_count)])

    listed = jnp.transpose(dispatched_entries[0], (2, 0, 1))
    packet, outgoing = call(
        prepare_body,
        [remote] * 4,
        (in_vmem(packet_shape), in_vmem(chunks)),
        [
            pltpu.VMEM(picture_features.shape, F32),
            pltpu.VMEM((1, image_rows), jnp.int32),
            pltpu.VMEM(caption_features_per_holder.shape, F32),
            pltpu.VMEM(listed.shape, jnp.int32),
            staging,
            pltpu.SemaphoreType.DMA((4,)),
        ],
        name="prepare",
    )(
        *[
            pltpu.with_memory_space_constraint(each, pltpu.HBM)
            for each in (
                picture_features,
                positive_caption_position.reshape(1, -1),
                caption_features_per_holder,
                listed,
            )
        ]
    )

    packet_two = passed_along(packet, "loop", -2)
    packet_relay = lax.ppermute(
        packet, "loop", [(source, (source - 3 + 2 * (source % 2)) % loop_count) for source in range(loop_count)]
    )
    incoming = lax.all_to_all(outgoing, "grp", split_axis=0, concat_axis=0, tiled=True)
    packet_swap = swapped(packet_two)

    block = call(assemble_kernel, [whole] * 2, in_vmem(block_shape), [staging, slot_rows], name="assemble")(
        incoming, sent_tally
    )
    block_two = passed_along(block, "loop", 2)

    sendback = call(
        text_kernel, [scalar] * 2 + [whole] * (2 + STOPS), in_vmem(chunks), [staging], name="text_grads", cost=big
    )(score_scale_factor, score_shift_term, sent_tally, block, packet, packet_two, packet_relay, packet_swap)
    returned = lax.all_to_all(sendback, "grp", split_axis=0, concat_axis=0, tiled=True)

    relayed_block = call(relay_kernel, [whole] * 2, in_vmem(block_shape), name="relay_blocks", cost=huge)(
        block, block_two
    )
    block_relay = passed_along(relayed_block, "loop", 1)
    block_swap = swapped(block_two)
    image_grad = call(
        image_kernel,
        [scalar] * 2 + [whole] * (1 + STOPS),
        jax.ShapeDtypeStruct((image_rows, features), F32),
        name="image_grads",
        cost=big,
    )(score_scale_factor, score_shift_term, packet, block, block_two, block_relay, block_swap)

    text_grad = call(
        return_kernel,
        [whole] * 3,
        jax.ShapeDtypeStruct((text_rows, features), F32),
        [staging, slot_rows],
        name="give_back",
    )(returned, listed, sent_tally)
    return (image_grad, text_grad)


def solution(mesh):
    placed = (
        P(("loop", "grp"), None),
        P(("loop", "grp"), None),
        P("loop", "grp", None, None),
        P("loop", None, None),
        P(("loop", "grp")),
        P(),
        P(),
    )
    return jax.shard_map(
        local,
        mesh=mesh,
        in_specs=placed,
        out_specs=(P(("loop", "grp"), None), P(("loop", "grp"), None)),
        check_vma=False,
    )
```

```python
import jax
import jax.numpy as jnp
from jax import lax
from jax.experimental import pallas as pl
from jax.experimental.pallas import tpu as pltpu
from jax.sharding import PartitionSpec as P

STOPS = 4
LANES = 128
AUX_ROWS = 16
PARTS = 4
WIDTH = 3 * LANES
BF16 = jnp.bfloat16
F32 = jnp.float32


def passed_along(value, axis, steps):
    count = lax.axis_size(axis)
    pairs = [(source, (source + steps) % count) for source in range(count)]
    return lax.ppermute(value, axis, pairs)


def iota(shape, dim):
    return lax.broadcasted_iota(jnp.int32, shape, dim)


def rows_to_chunks(rows, staging, chunks_ref, chunks_hbm, sent):
    peers, chunk_rows, _ = chunks_ref.shape
    pitch = staging.shape[0] // peers
    tiles = rows.shape[1] // LANES
    for slot in range(rows.shape[0] // peers):
        for tile in range(tiles):
            staging[pl.ds(slot * tiles + tile, peers, stride=pitch), :] = rows[
                slot * peers : (slot + 1) * peers, tile * LANES : (tile + 1) * LANES
            ]
    group = peers // PARTS
    copies = []
    for part in range(PARTS):
        for peer in range(part * group, (part + 1) * group):
            chunks_ref[peer] = staging[peer * pitch : peer * pitch + chunk_rows, :].astype(chunks_ref.dtype)
        at = pl.ds(part * group, group)
        copies.append(pltpu.make_async_copy(chunks_ref.at[at], chunks_hbm.at[at], sent.at[part]))
        copies[-1].start()
    return copies


def chunks_to_rows(chunks_ref, staging, rows_ref):
    peers, chunk_rows, _ = chunks_ref.shape
    pitch = staging.shape[0] // peers
    tiles = rows_ref.shape[1] // LANES
    for peer in range(peers):
        staging[peer * pitch : peer * pitch + chunk_rows, :] = chunks_ref[peer].astype(F32)
    for slot in range(rows_ref.shape[0] // peers):
        for tile in range(tiles):
            rows_ref[slot * peers : (slot + 1) * peers, tile * LANES : (tile + 1) * LANES] = staging[
                pl.ds(slot * tiles + tile, peers, stride=pitch), :
            ].astype(rows_ref.dtype)


def hits(columns, width):
    return jnp.concatenate(
        [(column == iota((column.shape[0], width), 1)).astype(F32) for column in columns], axis=0
    ).astype(BF16)


def upright(listed_ref):
    peers = listed_ref.shape[2]
    diagonal = iota((peers, peers), 0) == iota((peers, peers), 1)
    return [
        jnp.sum(jnp.where(diagonal, listed_ref[slot], 0), axis=1, keepdims=True) for slot in range(listed_ref.shape[0])
    ]


def block_places(tally, group_at, slot_cap, width):
    peers = tally.shape[0]
    mine = jnp.where(iota(tally.shape, 1) == group_at, tally, 0)
    before = (iota((peers, peers), 1) < iota((peers, peers), 0)).astype(F32)
    starts = jnp.dot(before, mine.astype(F32), preferred_element_type=F32)
    incoming = jnp.sum(mine, axis=1, keepdims=True)
    first = jnp.sum(starts, axis=1, keepdims=True).astype(jnp.int32)
    return hits([jnp.where(incoming > slot, first + slot, -1) for slot in range(slot_cap)], width)


def places_of(packet_ref, stop):
    rows = packet_ref.shape[0] - AUX_ROWS
    kept = packet_ref[rows:, 0:rows].astype(F32)
    return jnp.sum(jnp.where(iota(kept.shape, 0) == stop, kept, 0.0), axis=0, keepdims=True).astype(jnp.int32)


def slopes_for(text, image, places, scale, shift):
    scores = lax.dot_general(text, image, (((1,), (1,)), ((), ())), preferred_element_type=F32)
    logits = scale * scores + shift
    positive = places == iota(scores.shape, 0)
    toward = jax.nn.sigmoid(jnp.where(positive, -logits, logits))
    return (jnp.where(positive, -scale, scale) * toward).astype(BF16)


def prepare_kernel(
    loop_count,
    group_count,
    picture_hbm,
    positive_hbm,
    caption_hbm,
    listed_hbm,
    packet_ref,
    chunks_hbm,
    picture_ref,
    positive_ref,
    caption_ref,
    listed_ref,
    staging,
    chunks_ref,
    arrived,
    sent,
):
    copies = [
        pltpu.make_async_copy(source, target, arrived.at[at])
        for at, (source, target) in enumerate(
            [
                (listed_hbm, listed_ref),
                (caption_hbm, caption_ref),
                (positive_hbm, positive_ref),
                (picture_hbm, picture_ref),
            ]
        )
    ]
    for copy in copies:
        copy.start()
    text_rows = caption_ref.shape[0]
    copies[0].wait()
    chosen = hits(upright(listed_ref), text_rows)
    copies[1].wait()
    gathered = jnp.dot(chosen, caption_ref[...].astype(BF16), preferred_element_type=F32)
    leaving = rows_to_chunks(gathered, staging, chunks_ref, chunks_hbm, sent)
    rows = picture_ref.shape[0]
    copies[2].wait()
    positive = positive_ref[...]
    anchor = positive // (group_count * text_rows)
    behind = lax.rem(lax.axis_index("loop") - anchor + loop_count, loop_count)
    place = lax.rem(positive, text_rows)
    packet_ref[rows:, :] = jnp.zeros((AUX_ROWS, packet_ref.shape[1]), BF16)
    packet_ref[rows:, 0:rows] = jnp.where(behind == iota((AUX_ROWS, rows), 0), place, -1).astype(F32).astype(BF16)
    copies[3].wait()
    packet_ref[0:rows, :] = picture_ref[...].astype(BF16)
    for copy in leaving:
        copy.wait()


def relay_kernel(own_ref, arrived_ref, out_ref):
    parity = lax.rem(lax.axis_index("loop"), 2)

    @pl.when(parity == 1)
    def _():
        out_ref[...] = arrived_ref[...]

    @pl.when(parity == 0)
    def _():
        out_ref[...] = own_ref[...]


def assemble_kernel(chunks_ref, tally_ref, block_ref, staging, rows_ref):
    slot_cap = rows_ref.shape[0] // chunks_ref.shape[0]
    chunks_to_rows(chunks_ref, staging, rows_ref)
    places = block_places(tally_ref[0], lax.axis_index("grp"), slot_cap, block_ref.shape[0])
    block_ref[...] = lax.dot_general(
        places, rows_ref[...], (((0,), (0,)), ((), ())), preferred_element_type=F32
    ).astype(BF16)


def text_kernel(scale_ref, shift_ref, block_ref, *refs):
    packets, grad_ref = refs[:STOPS], refs[STOPS]
    scale, shift = scale_ref[0], shift_ref[0]
    text = block_ref[...]
    rows = packets[0].shape[0] - AUX_ROWS
    odd = lax.rem(lax.axis_index("loop"), 2)
    total = jnp.zeros(text.shape, F32)
    for stop, packet in zip((0, 2, 1 + 2 * odd, 3 - 2 * odd), packets):
        image = packet[0:rows, :]
        slopes = slopes_for(text, image, places_of(packet, stop), scale, shift)
        total = total + jnp.dot(slopes, image, preferred_element_type=F32)
    grad_ref[...] = total.astype(BF16)


def send_kernel(tally_ref, grad_ref, chunks_hbm, staging, chunks_ref, sent):
    rows, width = grad_ref.shape
    slot_cap = chunks_ref.shape[1] * LANES // width
    slots = block_places(tally_ref[0], lax.axis_index("grp"), slot_cap, rows)
    gathered = jnp.dot(slots, grad_ref[...], preferred_element_type=F32)
    for copy in rows_to_chunks(gathered, staging, chunks_ref, chunks_hbm, sent):
        copy.wait()


def column_copies(source_ref, target_hbm, sent):
    return [
        pltpu.make_async_copy(
            source_ref.at[:, pl.ds(start, WIDTH)], target_hbm.at[:, pl.ds(start, WIDTH)], sent.at[start // WIDTH]
        )
        for start in range(0, source_ref.shape[1], WIDTH)
    ]


def image_kernel(scale_ref, shift_ref, packet_ref, *refs):
    blocks, grad_hbm, grad_ref, sent = refs[:STOPS], *refs[STOPS:]
    scale, shift = scale_ref[0], shift_ref[0]
    rows = grad_ref.shape[0]
    image = packet_ref[0:rows, :]
    odd = lax.rem(lax.axis_index("loop"), 2)
    slopes = [
        slopes_for(block[...], image, places_of(packet_ref, stop), scale, shift)
        for stop, block in zip((0, 2, 3 - 2 * odd, 1 + 2 * odd), blocks)
    ]
    copies = column_copies(grad_ref, grad_hbm, sent)
    for part, copy in enumerate(copies):
        columns = slice(part * WIDTH, (part + 1) * WIDTH)
        total = None
        for slope, block in zip(slopes, blocks):
            term = lax.dot_general(slope, block[:, columns], (((0,), (0,)), ((), ())), preferred_element_type=F32)
            total = term if total is None else total + term
        grad_ref[:, columns] = total
        copy.start()
    for copy in copies:
        copy.wait()


def return_kernel(chunks_ref, listed_ref, tally_ref, grad_hbm, staging, rows_ref, grad_ref, sent):
    chunks_to_rows(chunks_ref, staging, rows_ref)
    tally = tally_ref[0]
    peers = tally.shape[0]
    mine = jnp.sum(jnp.where(iota(tally.shape, 0) == lax.axis_index("grp"), tally, 0), axis=0, keepdims=True)
    diagonal = iota((peers, peers), 0) == iota((peers, peers), 1)
    outgoing = jnp.sum(jnp.where(diagonal, mine, 0), axis=1, keepdims=True)
    owned = hits(
        [jnp.where(outgoing > slot, rows, -1) for slot, rows in enumerate(upright(listed_ref))], grad_ref.shape[0]
    )
    copies = column_copies(grad_ref, grad_hbm, sent)
    for part, copy in enumerate(copies):
        columns = slice(part * WIDTH, (part + 1) * WIDTH)
        grad_ref[:, columns] = lax.dot_general(
            owned, rows_ref[:, columns], (((0,), (0,)), ((), ())), preferred_element_type=F32
        )
        copy.start()
    for copy in copies:
        copy.wait()


def local(
    picture_features,
    caption_features_per_holder,
    dispatched_entries,
    sent_tally,
    positive_caption_position,
    score_scale_factor,
    score_shift_term,
):
    group_count = lax.axis_size("grp")
    loop_count = lax.axis_size("loop")
    image_rows, features = picture_features.shape
    text_rows = caption_features_per_holder.shape[0]
    slot_cap = dispatched_entries.shape[3]
    chunk_rows = slot_cap * features // LANES
    pitch = -(-chunk_rows // 8) * 8

    whole = pl.BlockSpec(memory_space=pltpu.VMEM)
    scalar = pl.BlockSpec(memory_space=pltpu.SMEM)
    remote = pl.BlockSpec(memory_space=pltpu.HBM)
    staging = pltpu.VMEM((group_count * pitch, LANES), F32)
    slot_rows = pltpu.VMEM((group_count * slot_cap, features), BF16)
    chunks = jax.ShapeDtypeStruct((group_count, chunk_rows, LANES), BF16)
    packet_shape = jax.ShapeDtypeStruct((image_rows + AUX_ROWS, features), BF16)
    big = pl.CostEstimate(flops=6 * STOPS * image_rows * text_rows * features, bytes_accessed=8 * image_rows * features, transcendentals=0)
    huge = pl.CostEstimate(flops=50 * 1000 * 1000 * 1000, bytes_accessed=0, transcendentals=0)
    block_shape = jax.ShapeDtypeStruct((text_rows, features), BF16)

    leaving = pltpu.VMEM(chunks.shape, BF16)
    column_sems = pltpu.SemaphoreType.DMA((features // WIDTH,))

    def in_vmem(shape):
        return pltpu.VMEM(shape.shape, shape.dtype)

    def call(kernel, in_specs, out_shape, scratch=(), name=None, cost=None, outs=None):
        return pl.pallas_call(
            kernel,
            out_shape=out_shape,
            in_specs=in_specs,
            out_specs=jax.tree.map(lambda _: whole, out_shape) if outs is None else outs,
            scratch_shapes=list(scratch),
            compiler_params=pltpu.CompilerParams(vmem_limit_bytes=24 * 1024 * 1024),
            name=name,
            cost_estimate=cost,
        )

    def prepare_body(*refs):
        prepare_kernel(loop_count, group_count, *refs)

    def swapped(value):
        return lax.ppermute(value, "loop", [(source, source ^ 1) for source in range(loop_count)])

    listed = jnp.transpose(dispatched_entries[0], (2, 0, 1))
    packet, outgoing = call(
        prepare_body,
        [remote] * 4,
        (in_vmem(packet_shape), chunks),
        [
            pltpu.VMEM(picture_features.shape, F32),
            pltpu.VMEM((1, image_rows), jnp.int32),
            pltpu.VMEM(caption_features_per_holder.shape, F32),
            pltpu.VMEM(listed.shape, jnp.int32),
            staging,
            leaving,
            pltpu.SemaphoreType.DMA((4,)),
            pltpu.SemaphoreType.DMA((PARTS,)),
        ],
        name="prepare",
        outs=(whole, remote),
    )(
        *[
            pltpu.with_memory_space_constraint(each, pltpu.HBM)
            for each in (
                picture_features,
                positive_caption_position.reshape(1, -1),
                caption_features_per_holder,
                listed,
            )
        ]
    )

    packet_two = passed_along(packet, "loop", -2)
    packet_relay = lax.ppermute(
        packet, "loop", [(source, (source - 3 + 2 * (source % 2)) % loop_count) for source in range(loop_count)]
    )
    incoming = lax.all_to_all(outgoing, "grp", split_axis=0, concat_axis=0, tiled=True)
    packet_swap = swapped(packet_two)

    block = call(assemble_kernel, [whole] * 2, in_vmem(block_shape), [staging, slot_rows], name="assemble")(
        incoming, sent_tally
    )

    block_grad = call(text_kernel, [scalar] * 2 + [whole] * (1 + STOPS), in_vmem(block_shape), name="text_grads")(
        score_scale_factor, score_shift_term, block, packet, packet_two, packet_relay, packet_swap
    )
    block_two = pltpu.with_memory_space_constraint(passed_along(block, "loop", 2), pltpu.VMEM)
    sendback = call(
        send_kernel,
        [whole] * 2,
        chunks,
        [staging, leaving, pltpu.SemaphoreType.DMA((PARTS,))],
        name="send_back",
        cost=huge,
        outs=remote,
    )(sent_tally, block_grad)
    returned = lax.all_to_all(sendback, "grp", split_axis=0, concat_axis=0, tiled=True)

    relayed_block = call(relay_kernel, [whole] * 2, in_vmem(block_shape), name="relay_blocks", cost=huge)(
        block, block_two
    )
    block_relay = passed_along(relayed_block, "loop", 1)
    block_swap = swapped(block_two)
    image_grad = call(
        image_kernel,
        [scalar] * 2 + [whole] * (1 + STOPS),
        jax.ShapeDtypeStruct((image_rows, features), F32),
        [pltpu.VMEM((image_rows, features), F32), column_sems],
        name="image_grads",
        cost=big,
        outs=remote,
    )(score_scale_factor, score_shift_term, packet, block, block_two, block_relay, block_swap)

    text_grad = call(
        return_kernel,
        [whole] * 3,
        jax.ShapeDtypeStruct((text_rows, features), F32),
        [staging, slot_rows, pltpu.VMEM((text_rows, features), F32), column_sems],
        name="give_back",
        outs=remote,
    )(returned, listed, sent_tally)
    return (image_grad, text_grad)


def solution(mesh):
    placed = (
        P(("loop", "grp"), None),
        P(("loop", "grp"), None),
        P("loop", "grp", None, None),
        P("loop", None, None),
        P(("loop", "grp")),
        P(),
        P(),
    )
    return jax.shard_map(
        local,
        mesh=mesh,
        in_specs=placed,
        out_specs=(P(("loop", "grp"), None), P(("loop", "grp"), None)),
        check_vma=False,
    )
```

```python
import jax
import jax.numpy as jnp
from jax import lax
from jax.experimental import pallas as pl
from jax.experimental.pallas import tpu as pltpu
from jax.sharding import PartitionSpec as P

STOPS = 4
LANES = 128
AUX_ROWS = 16
PARTS = 4
WIDTH = 3 * LANES
BF16 = jnp.bfloat16
F32 = jnp.float32


def passed_along(value, axis, steps):
    count = lax.axis_size(axis)
    pairs = [(source, (source + steps) % count) for source in range(count)]
    return lax.ppermute(value, axis, pairs)


def iota(shape, dim):
    return lax.broadcasted_iota(jnp.int32, shape, dim)


def rows_to_chunks(rows, staging, chunks_ref, chunks_hbm, sent):
    peers, chunk_rows, _ = chunks_ref.shape
    pitch = staging.shape[0] // peers
    tiles = rows.shape[1] // LANES
    for slot in range(rows.shape[0] // peers):
        for tile in range(tiles):
            staging[pl.ds(slot * tiles + tile, peers, stride=pitch), :] = rows[
                slot * peers : (slot + 1) * peers, tile * LANES : (tile + 1) * LANES
            ]
    group = peers // PARTS
    copies = []
    for part in range(PARTS):
        for peer in range(part * group, (part + 1) * group):
            chunks_ref[peer] = staging[peer * pitch : peer * pitch + chunk_rows, :].astype(chunks_ref.dtype)
        at = pl.ds(part * group, group)
        copies.append(pltpu.make_async_copy(chunks_ref.at[at], chunks_hbm.at[at], sent.at[part]))
        copies[-1].start()
    return copies


def chunks_to_rows(chunks_ref, staging, rows_ref):
    peers, chunk_rows, _ = chunks_ref.shape
    pitch = staging.shape[0] // peers
    tiles = rows_ref.shape[1] // LANES
    for peer in range(peers):
        staging[peer * pitch : peer * pitch + chunk_rows, :] = chunks_ref[peer].astype(F32)
    for slot in range(rows_ref.shape[0] // peers):
        for tile in range(tiles):
            rows_ref[slot * peers : (slot + 1) * peers, tile * LANES : (tile + 1) * LANES] = staging[
                pl.ds(slot * tiles + tile, peers, stride=pitch), :
            ].astype(rows_ref.dtype)


def hits(columns, width):
    return jnp.concatenate(
        [(column == iota((column.shape[0], width), 1)).astype(F32) for column in columns], axis=0
    ).astype(BF16)


def upright(listed_ref):
    peers = listed_ref.shape[2]
    diagonal = iota((peers, peers), 0) == iota((peers, peers), 1)
    return [
        jnp.sum(jnp.where(diagonal, listed_ref[slot], 0), axis=1, keepdims=True) for slot in range(listed_ref.shape[0])
    ]


def block_places(tally, group_at, slot_cap, width):
    peers = tally.shape[0]
    mine = jnp.where(iota(tally.shape, 1) == group_at, tally, 0)
    before = (iota((peers, peers), 1) < iota((peers, peers), 0)).astype(F32)
    starts = jnp.dot(before, mine.astype(F32), preferred_element_type=F32)
    incoming = jnp.sum(mine, axis=1, keepdims=True)
    first = jnp.sum(starts, axis=1, keepdims=True).astype(jnp.int32)
    return hits([jnp.where(incoming > slot, first + slot, -1) for slot in range(slot_cap)], width)


def places_of(packet_ref, stop):
    rows = packet_ref.shape[0] - AUX_ROWS
    kept = packet_ref[rows:, 0:rows].astype(F32)
    return jnp.sum(jnp.where(iota(kept.shape, 0) == stop, kept, 0.0), axis=0, keepdims=True).astype(jnp.int32)


def slopes_for(text, image, places, scale, shift):
    scores = lax.dot_general(text, image, (((1,), (1,)), ((), ())), preferred_element_type=F32)
    logits = scale * scores + shift
    positive = places == iota(scores.shape, 0)
    toward = jax.nn.sigmoid(jnp.where(positive, -logits, logits))
    return (jnp.where(positive, -scale, scale) * toward).astype(BF16)


def prepare_kernel(
    loop_count,
    group_count,
    picture_hbm,
    positive_hbm,
    caption_hbm,
    listed_hbm,
    packet_ref,
    chunks_hbm,
    picture_ref,
    positive_ref,
    caption_ref,
    listed_ref,
    staging,
    chunks_ref,
    arrived,
    sent,
):
    copies = [
        pltpu.make_async_copy(source, target, arrived.at[at])
        for at, (source, target) in enumerate(
            [
                (listed_hbm, listed_ref),
                (caption_hbm, caption_ref),
                (positive_hbm, positive_ref),
                (picture_hbm, picture_ref),
            ]
        )
    ]
    for copy in copies:
        copy.start()
    text_rows = caption_ref.shape[0]
    copies[0].wait()
    chosen = hits(upright(listed_ref), text_rows)
    copies[1].wait()
    gathered = jnp.dot(chosen, caption_ref[...].astype(BF16), preferred_element_type=F32)
    leaving = rows_to_chunks(gathered, staging, chunks_ref, chunks_hbm, sent)
    rows = picture_ref.shape[0]
    copies[2].wait()
    positive = positive_ref[...]
    anchor = positive // (group_count * text_rows)
    behind = lax.rem(lax.axis_index("loop") - anchor + loop_count, loop_count)
    place = lax.rem(positive, text_rows)
    packet_ref[rows:, :] = jnp.zeros((AUX_ROWS, packet_ref.shape[1]), BF16)
    packet_ref[rows:, 0:rows] = jnp.where(behind == iota((AUX_ROWS, rows), 0), place, -1).astype(F32).astype(BF16)
    copies[3].wait()
    packet_ref[0:rows, :] = picture_ref[...].astype(BF16)
    for copy in leaving:
        copy.wait()


def relay_kernel(passing, own_ref, arrived_ref, out_ref):
    parity = lax.rem(lax.axis_index("loop"), 2)

    @pl.when(parity == passing)
    def _():
        out_ref[...] = arrived_ref[...]

    @pl.when(parity != passing)
    def _():
        out_ref[...] = own_ref[...]


def assemble_kernel(chunks_ref, tally_ref, block_ref, staging, rows_ref):
    slot_cap = rows_ref.shape[0] // chunks_ref.shape[0]
    chunks_to_rows(chunks_ref, staging, rows_ref)
    places = block_places(tally_ref[0], lax.axis_index("grp"), slot_cap, block_ref.shape[0])
    block_ref[...] = lax.dot_general(
        places, rows_ref[...], (((0,), (0,)), ((), ())), preferred_element_type=F32
    ).astype(BF16)


def text_kernel(scale_ref, shift_ref, block_ref, *refs):
    packets, grad_ref = refs[:STOPS], refs[STOPS]
    scale, shift = scale_ref[0], shift_ref[0]
    text = block_ref[...]
    rows = packets[0].shape[0] - AUX_ROWS
    odd = lax.rem(lax.axis_index("loop"), 2)
    total = jnp.zeros(text.shape, F32)
    for stop, packet in zip((0, 2, 1 + 2 * odd, 3 - 2 * odd), packets):
        image = packet[0:rows, :]
        slopes = slopes_for(text, image, places_of(packet, stop), scale, shift)
        total = total + jnp.dot(slopes, image, preferred_element_type=F32)
    grad_ref[...] = total.astype(BF16)


def send_kernel(tally_ref, grad_ref, chunks_hbm, staging, chunks_ref, sent):
    rows, width = grad_ref.shape
    slot_cap = chunks_ref.shape[1] * LANES // width
    slots = block_places(tally_ref[0], lax.axis_index("grp"), slot_cap, rows)
    gathered = jnp.dot(slots, grad_ref[...], preferred_element_type=F32)
    for copy in rows_to_chunks(gathered, staging, chunks_ref, chunks_hbm, sent):
        copy.wait()


def column_copies(source_ref, target_hbm, sent):
    return [
        pltpu.make_async_copy(
            source_ref.at[:, pl.ds(start, WIDTH)], target_hbm.at[:, pl.ds(start, WIDTH)], sent.at[start // WIDTH]
        )
        for start in range(0, source_ref.shape[1], WIDTH)
    ]


def image_kernel(scale_ref, shift_ref, packet_ref, *refs):
    blocks, grad_hbm, grad_ref, sent = refs[:STOPS], *refs[STOPS:]
    scale, shift = scale_ref[0], shift_ref[0]
    rows = grad_ref.shape[0]
    image = packet_ref[0:rows, :]
    odd = lax.rem(lax.axis_index("loop"), 2)
    slopes = [
        slopes_for(block[...], image, places_of(packet_ref, stop), scale, shift)
        for stop, block in zip((0, 2, 3 - 2 * odd, 1 + 2 * odd), blocks)
    ]
    copies = column_copies(grad_ref, grad_hbm, sent)
    for part, copy in enumerate(copies):
        columns = slice(part * WIDTH, (part + 1) * WIDTH)
        total = None
        for slope, block in zip(slopes, blocks):
            term = lax.dot_general(slope, block[:, columns], (((0,), (0,)), ((), ())), preferred_element_type=F32)
            total = term if total is None else total + term
        grad_ref[:, columns] = total
        copy.start()
    for copy in copies:
        copy.wait()


def return_kernel(chunks_ref, listed_ref, tally_ref, grad_hbm, staging, rows_ref, grad_ref, sent):
    chunks_to_rows(chunks_ref, staging, rows_ref)
    tally = tally_ref[0]
    peers = tally.shape[0]
    mine = jnp.sum(jnp.where(iota(tally.shape, 0) == lax.axis_index("grp"), tally, 0), axis=0, keepdims=True)
    diagonal = iota((peers, peers), 0) == iota((peers, peers), 1)
    outgoing = jnp.sum(jnp.where(diagonal, mine, 0), axis=1, keepdims=True)
    owned = hits(
        [jnp.where(outgoing > slot, rows, -1) for slot, rows in enumerate(upright(listed_ref))], grad_ref.shape[0]
    )
    copies = column_copies(grad_ref, grad_hbm, sent)
    for part, copy in enumerate(copies):
        columns = slice(part * WIDTH, (part + 1) * WIDTH)
        grad_ref[:, columns] = lax.dot_general(
            owned, rows_ref[:, columns], (((0,), (0,)), ((), ())), preferred_element_type=F32
        )
        copy.start()
    for copy in copies:
        copy.wait()


def local(
    picture_features,
    caption_features_per_holder,
    dispatched_entries,
    sent_tally,
    positive_caption_position,
    score_scale_factor,
    score_shift_term,
):
    group_count = lax.axis_size("grp")
    loop_count = lax.axis_size("loop")
    image_rows, features = picture_features.shape
    text_rows = caption_features_per_holder.shape[0]
    slot_cap = dispatched_entries.shape[3]
    chunk_rows = slot_cap * features // LANES
    pitch = -(-chunk_rows // 8) * 8

    whole = pl.BlockSpec(memory_space=pltpu.VMEM)
    scalar = pl.BlockSpec(memory_space=pltpu.SMEM)
    remote = pl.BlockSpec(memory_space=pltpu.HBM)
    staging = pltpu.VMEM((group_count * pitch, LANES), F32)
    slot_rows = pltpu.VMEM((group_count * slot_cap, features), BF16)
    chunks = jax.ShapeDtypeStruct((group_count, chunk_rows, LANES), BF16)
    packet_shape = jax.ShapeDtypeStruct((image_rows + AUX_ROWS, features), BF16)
    big = pl.CostEstimate(flops=6 * STOPS * image_rows * text_rows * features, bytes_accessed=8 * image_rows * features, transcendentals=0)
    huge = pl.CostEstimate(flops=50 * 1000 * 1000 * 1000, bytes_accessed=0, transcendentals=0)
    block_shape = jax.ShapeDtypeStruct((text_rows, features), BF16)

    leaving = pltpu.VMEM(chunks.shape, BF16)
    column_sems = pltpu.SemaphoreType.DMA((features // WIDTH,))

    def in_vmem(shape):
        return pltpu.VMEM(shape.shape, shape.dtype)

    def call(kernel, in_specs, out_shape, scratch=(), name=None, cost=None, outs=None):
        return pl.pallas_call(
            kernel,
            out_shape=out_shape,
            in_specs=in_specs,
            out_specs=jax.tree.map(lambda _: whole, out_shape) if outs is None else outs,
            scratch_shapes=list(scratch),
            compiler_params=pltpu.CompilerParams(vmem_limit_bytes=24 * 1024 * 1024),
            name=name,
            cost_estimate=cost,
        )

    def prepare_body(*refs):
        prepare_kernel(loop_count, group_count, *refs)

    def keep_even(*refs):
        relay_kernel(0, *refs)

    def keep_odd(*refs):
        relay_kernel(1, *refs)

    def swapped(value):
        return lax.ppermute(value, "loop", [(source, source ^ 1) for source in range(loop_count)])

    listed = jnp.transpose(dispatched_entries[0], (2, 0, 1))
    packet, outgoing = call(
        prepare_body,
        [remote] * 4,
        (in_vmem(packet_shape), chunks),
        [
            pltpu.VMEM(picture_features.shape, F32),
            pltpu.VMEM((1, image_rows), jnp.int32),
            pltpu.VMEM(caption_features_per_holder.shape, F32),
            pltpu.VMEM(listed.shape, jnp.int32),
            staging,
            leaving,
            pltpu.SemaphoreType.DMA((4,)),
            pltpu.SemaphoreType.DMA((PARTS,)),
        ],
        name="prepare",
        outs=(whole, remote),
    )(
        *[
            pltpu.with_memory_space_constraint(each, pltpu.HBM)
            for each in (
                picture_features,
                positive_caption_position.reshape(1, -1),
                caption_features_per_holder,
                listed,
            )
        ]
    )

    packet_two = passed_along(packet, "loop", -2)
    incoming = lax.all_to_all(outgoing, "grp", split_axis=0, concat_axis=0, tiled=True)
    packet_swap = swapped(packet_two)
    relayed = call(keep_even, [whole] * 2, in_vmem(packet_shape), name="relay_images")(packet, packet_two)
    packet_relay = passed_along(relayed, "loop", -1)

    block = call(assemble_kernel, [whole] * 2, in_vmem(block_shape), [staging, slot_rows], name="assemble")(
        incoming, sent_tally
    )

    block_grad = call(text_kernel, [scalar] * 2 + [whole] * (1 + STOPS), in_vmem(block_shape), name="text_grads")(
        score_scale_factor, score_shift_term, block, packet, packet_two, packet_relay, packet_swap
    )
    block_two = pltpu.with_memory_space_constraint(passed_along(block, "loop", 2), pltpu.VMEM)
    sendback = call(
        send_kernel,
        [whole] * 2,
        chunks,
        [staging, leaving, pltpu.SemaphoreType.DMA((PARTS,))],
        name="send_back",
        cost=huge,
        outs=remote,
    )(sent_tally, block_grad)
    returned = lax.all_to_all(sendback, "grp", split_axis=0, concat_axis=0, tiled=True)

    relayed_block = call(keep_odd, [whole] * 2, in_vmem(block_shape), name="relay_blocks", cost=huge)(
        block, block_two
    )
    block_relay = passed_along(relayed_block, "loop", 1)
    block_swap = swapped(block_two)
    image_grad = call(
        image_kernel,
        [scalar] * 2 + [whole] * (1 + STOPS),
        jax.ShapeDtypeStruct((image_rows, features), F32),
        [pltpu.VMEM((image_rows, features), F32), column_sems],
        name="image_grads",
        cost=big,
        outs=remote,
    )(score_scale_factor, score_shift_term, packet, block, block_two, block_relay, block_swap)

    text_grad = call(
        return_kernel,
        [whole] * 3,
        jax.ShapeDtypeStruct((text_rows, features), F32),
        [staging, slot_rows, pltpu.VMEM((text_rows, features), F32), column_sems],
        name="give_back",
        outs=remote,
    )(returned, listed, sent_tally)
    return (image_grad, text_grad)


def solution(mesh):
    placed = (
        P(("loop", "grp"), None),
        P(("loop", "grp"), None),
        P("loop", "grp", None, None),
        P("loop", None, None),
        P(("loop", "grp")),
        P(),
        P(),
    )
    return jax.shard_map(
        local,
        mesh=mesh,
        in_specs=placed,
        out_specs=(P(("loop", "grp"), None), P(("loop", "grp"), None)),
        check_vma=False,
    )
```

```python
import jax
import jax.numpy as jnp
from jax import lax
from jax.experimental import pallas as pl
from jax.experimental.pallas import tpu as pltpu
from jax.sharding import PartitionSpec as P

STOPS = 4
LANES = 128
AUX_ROWS = 16
PARTS = 4
WIDTH = 3 * LANES
BF16 = jnp.bfloat16
F32 = jnp.float32


def passed_along(value, axis, steps):
    count = lax.axis_size(axis)
    pairs = [(source, (source + steps) % count) for source in range(count)]
    return lax.ppermute(value, axis, pairs)


def iota(shape, dim):
    return lax.broadcasted_iota(jnp.int32, shape, dim)


def rows_to_chunks(rows, staging, chunks_ref, chunks_hbm, sent):
    peers, chunk_rows, _ = chunks_ref.shape
    pitch = staging.shape[0] // peers
    tiles = rows.shape[1] // LANES
    for slot in range(rows.shape[0] // peers):
        for tile in range(tiles):
            staging[pl.ds(slot * tiles + tile, peers, stride=pitch), :] = rows[
                slot * peers : (slot + 1) * peers, tile * LANES : (tile + 1) * LANES
            ]
    group = peers // PARTS
    copies = []
    for part in range(PARTS):
        for peer in range(part * group, (part + 1) * group):
            chunks_ref[peer] = staging[peer * pitch : peer * pitch + chunk_rows, :].astype(chunks_ref.dtype)
        at = pl.ds(part * group, group)
        copies.append(pltpu.make_async_copy(chunks_ref.at[at], chunks_hbm.at[at], sent.at[part]))
        copies[-1].start()
    return copies


def chunks_to_rows(chunks_ref, staging, rows_ref):
    peers, chunk_rows, _ = chunks_ref.shape
    pitch = staging.shape[0] // peers
    tiles = rows_ref.shape[1] // LANES
    for peer in range(peers):
        staging[peer * pitch : peer * pitch + chunk_rows, :] = chunks_ref[peer].astype(F32)
    for slot in range(rows_ref.shape[0] // peers):
        for tile in range(tiles):
            rows_ref[slot * peers : (slot + 1) * peers, tile * LANES : (tile + 1) * LANES] = staging[
                pl.ds(slot * tiles + tile, peers, stride=pitch), :
            ].astype(rows_ref.dtype)


def hits(columns, width):
    return jnp.concatenate(
        [(column == iota((column.shape[0], width), 1)).astype(F32) for column in columns], axis=0
    ).astype(BF16)


def upright(listed_ref):
    peers = listed_ref.shape[2]
    diagonal = iota((peers, peers), 0) == iota((peers, peers), 1)
    return [
        jnp.sum(jnp.where(diagonal, listed_ref[slot], 0), axis=1, keepdims=True) for slot in range(listed_ref.shape[0])
    ]


def block_places(tally, group_at, slot_cap, width):
    peers = tally.shape[0]
    mine = jnp.where(iota(tally.shape, 1) == group_at, tally, 0)
    before = (iota((peers, peers), 1) < iota((peers, peers), 0)).astype(F32)
    starts = jnp.dot(before, mine.astype(F32), preferred_element_type=F32)
    incoming = jnp.sum(mine, axis=1, keepdims=True)
    first = jnp.sum(starts, axis=1, keepdims=True).astype(jnp.int32)
    return hits([jnp.where(incoming > slot, first + slot, -1) for slot in range(slot_cap)], width)


def places_of(packet_ref, stop):
    rows = packet_ref.shape[0] - AUX_ROWS
    kept = packet_ref[rows:, 0:rows].astype(F32)
    return jnp.sum(jnp.where(iota(kept.shape, 0) == stop, kept, 0.0), axis=0, keepdims=True).astype(jnp.int32)


def slopes_for(text, image, places, scale, shift):
    scores = lax.dot_general(text, image, (((1,), (1,)), ((), ())), preferred_element_type=F32)
    logits = scale * scores + shift
    positive = places == iota(scores.shape, 0)
    toward = jax.nn.sigmoid(jnp.where(positive, -logits, logits))
    return (jnp.where(positive, -scale, scale) * toward).astype(BF16)


def prepare_kernel(
    loop_count,
    group_count,
    picture_hbm,
    positive_hbm,
    caption_hbm,
    listed_hbm,
    packet_ref,
    chunks_hbm,
    picture_ref,
    positive_ref,
    caption_ref,
    listed_ref,
    staging,
    chunks_ref,
    arrived,
    sent,
):
    copies = [
        pltpu.make_async_copy(source, target, arrived.at[at])
        for at, (source, target) in enumerate(
            [
                (listed_hbm, listed_ref),
                (caption_hbm, caption_ref),
                (positive_hbm, positive_ref),
                (picture_hbm, picture_ref),
            ]
        )
    ]
    for copy in copies:
        copy.start()
    text_rows = caption_ref.shape[0]
    copies[0].wait()
    chosen = hits(upright(listed_ref), text_rows)
    copies[1].wait()
    gathered = jnp.dot(chosen, caption_ref[...].astype(BF16), preferred_element_type=F32)
    leaving = rows_to_chunks(gathered, staging, chunks_ref, chunks_hbm, sent)
    rows = picture_ref.shape[0]
    copies[2].wait()
    positive = positive_ref[...]
    anchor = positive // (group_count * text_rows)
    behind = lax.rem(lax.axis_index("loop") - anchor + loop_count, loop_count)
    place = lax.rem(positive, text_rows)
    packet_ref[rows:, :] = jnp.zeros((AUX_ROWS, packet_ref.shape[1]), BF16)
    packet_ref[rows:, 0:rows] = jnp.where(behind == iota((AUX_ROWS, rows), 0), place, -1).astype(F32).astype(BF16)
    copies[3].wait()
    packet_ref[0:rows, :] = picture_ref[...].astype(BF16)
    for copy in leaving:
        copy.wait()


def relay_kernel(passing, own_ref, arrived_ref, out_ref):
    parity = lax.rem(lax.axis_index("loop"), 2)

    @pl.when(parity == passing)
    def _():
        out_ref[...] = arrived_ref[...]

    @pl.when(parity != passing)
    def _():
        out_ref[...] = own_ref[...]


def assemble_kernel(chunks_ref, tally_ref, block_ref, staging, rows_ref):
    slot_cap = rows_ref.shape[0] // chunks_ref.shape[0]
    chunks_to_rows(chunks_ref, staging, rows_ref)
    places = block_places(tally_ref[0], lax.axis_index("grp"), slot_cap, block_ref.shape[0])
    block_ref[...] = lax.dot_general(
        places, rows_ref[...], (((0,), (0,)), ((), ())), preferred_element_type=F32
    ).astype(BF16)


def text_kernel(scale_ref, shift_ref, block_ref, *refs):
    packets, grad_ref = refs[:STOPS], refs[STOPS]
    scale, shift = scale_ref[0], shift_ref[0]
    text = block_ref[...]
    rows = packets[0].shape[0] - AUX_ROWS
    odd = lax.rem(lax.axis_index("loop"), 2)
    slopes = [
        slopes_for(text, packet[0:rows, :], places_of(packet, stop), scale, shift)
        for stop, packet in zip((0, 2, 1 + 2 * odd, 3 - 2 * odd), packets)
    ]
    for start in range(0, text.shape[1], WIDTH):
        total = None
        for slope, packet in zip(slopes, packets):
            term = jnp.dot(slope, packet[0:rows, start : start + WIDTH], preferred_element_type=F32)
            total = term if total is None else total + term
        grad_ref[:, start : start + WIDTH] = total.astype(BF16)


def send_kernel(tally_ref, grad_ref, chunks_hbm, staging, chunks_ref, sent):
    rows, width = grad_ref.shape
    slot_cap = chunks_ref.shape[1] * LANES // width
    slots = block_places(tally_ref[0], lax.axis_index("grp"), slot_cap, rows)
    gathered = jnp.dot(slots, grad_ref[...], preferred_element_type=F32)
    for copy in rows_to_chunks(gathered, staging, chunks_ref, chunks_hbm, sent):
        copy.wait()


def column_copies(source_ref, target_hbm, sent):
    return [
        pltpu.make_async_copy(
            source_ref.at[:, pl.ds(start, WIDTH)], target_hbm.at[:, pl.ds(start, WIDTH)], sent.at[start // WIDTH]
        )
        for start in range(0, source_ref.shape[1], WIDTH)
    ]


def image_kernel(scale_ref, shift_ref, packet_ref, *refs):
    blocks, grad_hbm, grad_ref, sent = refs[:STOPS], *refs[STOPS:]
    scale, shift = scale_ref[0], shift_ref[0]
    rows = grad_ref.shape[0]
    image = packet_ref[0:rows, :]
    odd = lax.rem(lax.axis_index("loop"), 2)
    slopes = [
        slopes_for(block[...], image, places_of(packet_ref, stop), scale, shift)
        for stop, block in zip((0, 2, 3 - 2 * odd, 1 + 2 * odd), blocks)
    ]
    copies = column_copies(grad_ref, grad_hbm, sent)
    for part, copy in enumerate(copies):
        columns = slice(part * WIDTH, (part + 1) * WIDTH)
        total = None
        for slope, block in zip(slopes, blocks):
            term = lax.dot_general(slope, block[:, columns], (((0,), (0,)), ((), ())), preferred_element_type=F32)
            total = term if total is None else total + term
        grad_ref[:, columns] = total
        copy.start()
    for copy in copies:
        copy.wait()


def return_kernel(chunks_ref, listed_ref, tally_ref, grad_hbm, staging, rows_ref, grad_ref, sent):
    chunks_to_rows(chunks_ref, staging, rows_ref)
    tally = tally_ref[0]
    peers = tally.shape[0]
    mine = jnp.sum(jnp.where(iota(tally.shape, 0) == lax.axis_index("grp"), tally, 0), axis=0, keepdims=True)
    diagonal = iota((peers, peers), 0) == iota((peers, peers), 1)
    outgoing = jnp.sum(jnp.where(diagonal, mine, 0), axis=1, keepdims=True)
    owned = hits(
        [jnp.where(outgoing > slot, rows, -1) for slot, rows in enumerate(upright(listed_ref))], grad_ref.shape[0]
    )
    copies = column_copies(grad_ref, grad_hbm, sent)
    for part, copy in enumerate(copies):
        columns = slice(part * WIDTH, (part + 1) * WIDTH)
        grad_ref[:, columns] = lax.dot_general(
            owned, rows_ref[:, columns], (((0,), (0,)), ((), ())), preferred_element_type=F32
        )
        copy.start()
    for copy in copies:
        copy.wait()


def local(
    picture_features,
    caption_features_per_holder,
    dispatched_entries,
    sent_tally,
    positive_caption_position,
    score_scale_factor,
    score_shift_term,
):
    group_count = lax.axis_size("grp")
    loop_count = lax.axis_size("loop")
    image_rows, features = picture_features.shape
    text_rows = caption_features_per_holder.shape[0]
    slot_cap = dispatched_entries.shape[3]
    chunk_rows = slot_cap * features // LANES
    pitch = -(-chunk_rows // 8) * 8

    whole = pl.BlockSpec(memory_space=pltpu.VMEM)
    scalar = pl.BlockSpec(memory_space=pltpu.SMEM)
    remote = pl.BlockSpec(memory_space=pltpu.HBM)
    staging = pltpu.VMEM((group_count * pitch, LANES), F32)
    slot_rows = pltpu.VMEM((group_count * slot_cap, features), BF16)
    chunks = jax.ShapeDtypeStruct((group_count, chunk_rows, LANES), BF16)
    packet_shape = jax.ShapeDtypeStruct((image_rows + AUX_ROWS, features), BF16)
    big = pl.CostEstimate(flops=6 * STOPS * image_rows * text_rows * features, bytes_accessed=8 * image_rows * features, transcendentals=0)
    huge = pl.CostEstimate(flops=50 * 1000 * 1000 * 1000, bytes_accessed=0, transcendentals=0)
    block_shape = jax.ShapeDtypeStruct((text_rows, features), BF16)

    leaving = pltpu.VMEM(chunks.shape, BF16)
    column_sems = pltpu.SemaphoreType.DMA((features // WIDTH,))

    def in_vmem(shape):
        return pltpu.VMEM(shape.shape, shape.dtype)

    def call(kernel, in_specs, out_shape, scratch=(), name=None, cost=None, outs=None):
        return pl.pallas_call(
            kernel,
            out_shape=out_shape,
            in_specs=in_specs,
            out_specs=jax.tree.map(lambda _: whole, out_shape) if outs is None else outs,
            scratch_shapes=list(scratch),
            compiler_params=pltpu.CompilerParams(vmem_limit_bytes=12 * 1024 * 1024),
            name=name,
            cost_estimate=cost,
        )

    def prepare_body(*refs):
        prepare_kernel(loop_count, group_count, *refs)

    def keep_even(*refs):
        relay_kernel(0, *refs)

    def keep_odd(*refs):
        relay_kernel(1, *refs)

    def swapped(value):
        return lax.ppermute(value, "loop", [(source, source ^ 1) for source in range(loop_count)])

    listed = jnp.transpose(dispatched_entries[0], (2, 0, 1))
    packet, outgoing = call(
        prepare_body,
        [remote] * 4,
        (in_vmem(packet_shape), chunks),
        [
            pltpu.VMEM(picture_features.shape, F32),
            pltpu.VMEM((1, image_rows), jnp.int32),
            pltpu.VMEM(caption_features_per_holder.shape, F32),
            pltpu.VMEM(listed.shape, jnp.int32),
            staging,
            leaving,
            pltpu.SemaphoreType.DMA((4,)),
            pltpu.SemaphoreType.DMA((PARTS,)),
        ],
        name="prepare",
        outs=(whole, remote),
    )(
        *[
            pltpu.with_memory_space_constraint(each, pltpu.HBM)
            for each in (
                picture_features,
                positive_caption_position.reshape(1, -1),
                caption_features_per_holder,
                listed,
            )
        ]
    )

    packet_two = passed_along(packet, "loop", -2)
    incoming = lax.all_to_all(outgoing, "grp", split_axis=0, concat_axis=0, tiled=True)
    packet_swap = swapped(packet_two)
    relayed = call(keep_even, [whole] * 2, in_vmem(packet_shape), name="relay_images")(packet, packet_two)
    packet_relay = passed_along(relayed, "loop", -1)

    block = call(assemble_kernel, [whole] * 2, in_vmem(block_shape), [staging, slot_rows], name="assemble")(
        incoming, sent_tally
    )

    block_grad = call(text_kernel, [scalar] * 2 + [whole] * (1 + STOPS), in_vmem(block_shape), name="text_grads")(
        score_scale_factor, score_shift_term, block, packet, packet_two, packet_relay, packet_swap
    )
    block_two = pltpu.with_memory_space_constraint(passed_along(block, "loop", 2), pltpu.VMEM)
    sendback = call(
        send_kernel,
        [whole] * 2,
        chunks,
        [staging, leaving, pltpu.SemaphoreType.DMA((PARTS,))],
        name="send_back",
        cost=huge,
        outs=remote,
    )(sent_tally, block_grad)
    returned = lax.all_to_all(sendback, "grp", split_axis=0, concat_axis=0, tiled=True)

    relayed_block = call(keep_odd, [whole] * 2, in_vmem(block_shape), name="relay_blocks", cost=huge)(
        block, block_two
    )
    block_relay = passed_along(relayed_block, "loop", 1)
    block_swap = swapped(block_two)
    image_grad = call(
        image_kernel,
        [scalar] * 2 + [whole] * (1 + STOPS),
        jax.ShapeDtypeStruct((image_rows, features), F32),
        [pltpu.VMEM((image_rows, features), F32), column_sems],
        name="image_grads",
        cost=big,
        outs=remote,
    )(score_scale_factor, score_shift_term, packet, block, block_two, block_relay, block_swap)

    text_grad = call(
        return_kernel,
        [whole] * 3,
        jax.ShapeDtypeStruct((text_rows, features), F32),
        [staging, slot_rows, pltpu.VMEM((text_rows, features), F32), column_sems],
        name="give_back",
        outs=remote,
    )(returned, listed, sent_tally)
    return (image_grad, text_grad)


def solution(mesh):
    placed = (
        P(("loop", "grp"), None),
        P(("loop", "grp"), None),
        P("loop", "grp", None, None),
        P("loop", None, None),
        P(("loop", "grp")),
        P(),
        P(),
    )
    return jax.shard_map(
        local,
        mesh=mesh,
        in_specs=placed,
        out_specs=(P(("loop", "grp"), None), P(("loop", "grp"), None)),
        check_vma=False,
    )
```

```python
import jax
import jax.numpy as jnp
from jax import lax
from jax.experimental import pallas as pl
from jax.experimental.pallas import tpu as pltpu
from jax.sharding import PartitionSpec as P

STOPS = 4
LANES = 128
AUX_ROWS = 16
PARTS = 4
WIDTH = 3 * LANES
BF16 = jnp.bfloat16
F32 = jnp.float32


def passed_along(value, axis, steps):
    count = lax.axis_size(axis)
    pairs = [(source, (source + steps) % count) for source in range(count)]
    return lax.ppermute(value, axis, pairs)


def iota(shape, dim):
    return lax.broadcasted_iota(jnp.int32, shape, dim)


def rows_to_chunks(rows, staging, chunks_ref, chunks_hbm, sent):
    peers, chunk_rows, _ = chunks_ref.shape
    pitch = staging.shape[0] // peers
    tiles = rows.shape[1] // LANES
    for slot in range(rows.shape[0] // peers):
        for tile in range(tiles):
            staging[pl.ds(slot * tiles + tile, peers, stride=pitch), :] = rows[
                slot * peers : (slot + 1) * peers, tile * LANES : (tile + 1) * LANES
            ]
    group = peers // PARTS
    copies = []
    for part in range(PARTS):
        for peer in range(part * group, (part + 1) * group):
            chunks_ref[peer] = staging[peer * pitch : peer * pitch + chunk_rows, :].astype(chunks_ref.dtype)
        at = pl.ds(part * group, group)
        copies.append(pltpu.make_async_copy(chunks_ref.at[at], chunks_hbm.at[at], sent.at[part]))
        copies[-1].start()
    return copies


def chunks_to_rows(chunks_ref, staging, rows_ref):
    peers, chunk_rows, _ = chunks_ref.shape
    pitch = staging.shape[0] // peers
    tiles = rows_ref.shape[1] // LANES
    for peer in range(peers):
        staging[peer * pitch : peer * pitch + chunk_rows, :] = chunks_ref[peer].astype(F32)
    for slot in range(rows_ref.shape[0] // peers):
        for tile in range(tiles):
            rows_ref[slot * peers : (slot + 1) * peers, tile * LANES : (tile + 1) * LANES] = staging[
                pl.ds(slot * tiles + tile, peers, stride=pitch), :
            ].astype(rows_ref.dtype)


def hits(columns, width):
    return jnp.concatenate(
        [(column == iota((column.shape[0], width), 1)).astype(F32) for column in columns], axis=0
    ).astype(BF16)


def upright(listed_ref):
    peers = listed_ref.shape[2]
    diagonal = iota((peers, peers), 0) == iota((peers, peers), 1)
    return [
        jnp.sum(jnp.where(diagonal, listed_ref[slot], 0), axis=1, keepdims=True) for slot in range(listed_ref.shape[0])
    ]


def block_places(tally, group_at, slot_cap, width):
    peers = tally.shape[0]
    mine = jnp.where(iota(tally.shape, 1) == group_at, tally, 0)
    before = (iota((peers, peers), 1) < iota((peers, peers), 0)).astype(F32)
    starts = jnp.dot(before, mine.astype(F32), preferred_element_type=F32)
    incoming = jnp.sum(mine, axis=1, keepdims=True)
    first = jnp.sum(starts, axis=1, keepdims=True).astype(jnp.int32)
    return hits([jnp.where(incoming > slot, first + slot, -1) for slot in range(slot_cap)], width)


def places_of(packet_ref, stop):
    rows = packet_ref.shape[0] - AUX_ROWS
    kept = packet_ref[rows:, 0:rows].astype(F32)
    return jnp.sum(jnp.where(iota(kept.shape, 0) == stop, kept, 0.0), axis=0, keepdims=True).astype(jnp.int32)


def owned_rows(listed_ref, tally, group_at, width):
    peers = tally.shape[0]
    mine = jnp.sum(jnp.where(iota(tally.shape, 0) == group_at, tally, 0), axis=0, keepdims=True)
    diagonal = iota((peers, peers), 0) == iota((peers, peers), 1)
    outgoing = jnp.sum(jnp.where(diagonal, mine, 0), axis=1, keepdims=True)
    return hits([jnp.where(outgoing > slot, rows, -1) for slot, rows in enumerate(upright(listed_ref))], width)


def slopes_for(text, image, places, scale, shift):
    scores = lax.dot_general(text, image, (((1,), (1,)), ((), ())), preferred_element_type=F32)
    logits = scale * scores + shift
    positive = places == iota(scores.shape, 0)
    toward = jax.nn.sigmoid(jnp.where(positive, -logits, logits))
    return (jnp.where(positive, -scale, scale) * toward).astype(BF16)


def prepare_kernel(
    loop_count,
    group_count,
    picture_hbm,
    positive_hbm,
    caption_hbm,
    listed_hbm,
    packet_ref,
    chunks_hbm,
    picture_ref,
    positive_ref,
    caption_ref,
    listed_ref,
    staging,
    chunks_ref,
    arrived,
    sent,
):
    copies = [
        pltpu.make_async_copy(source, target, arrived.at[at])
        for at, (source, target) in enumerate(
            [
                (listed_hbm, listed_ref),
                (caption_hbm, caption_ref),
                (positive_hbm, positive_ref),
                (picture_hbm, picture_ref),
            ]
        )
    ]
    for copy in copies:
        copy.start()
    text_rows = caption_ref.shape[0]
    copies[0].wait()
    chosen = hits(upright(listed_ref), text_rows)
    copies[1].wait()
    gathered = jnp.dot(chosen, caption_ref[...].astype(BF16), preferred_element_type=F32)
    leaving = rows_to_chunks(gathered, staging, chunks_ref, chunks_hbm, sent)
    rows = picture_ref.shape[0]
    copies[2].wait()
    positive = positive_ref[...]
    anchor = positive // (group_count * text_rows)
    behind = lax.rem(lax.axis_index("loop") - anchor + loop_count, loop_count)
    place = lax.rem(positive, text_rows)
    packet_ref[rows:, :] = jnp.zeros((AUX_ROWS, packet_ref.shape[1]), BF16)
    packet_ref[rows:, 0:rows] = jnp.where(behind == iota((AUX_ROWS, rows), 0), place, -1).astype(F32).astype(BF16)
    copies[3].wait()
    packet_ref[0:rows, :] = picture_ref[...].astype(BF16)
    for copy in leaving:
        copy.wait()


def relay_kernel(passing, own_ref, arrived_ref, out_ref):
    parity = lax.rem(lax.axis_index("loop"), 2)

    @pl.when(parity == passing)
    def _():
        out_ref[...] = arrived_ref[...]

    @pl.when(parity != passing)
    def _():
        out_ref[...] = own_ref[...]


def assemble_kernel(chunks_ref, tally_ref, block_ref, places_ref, staging, rows_ref):
    slot_cap = rows_ref.shape[0] // chunks_ref.shape[0]
    chunks_to_rows(chunks_ref, staging, rows_ref)
    places = block_places(tally_ref[0], lax.axis_index("grp"), slot_cap, block_ref.shape[0])
    places_ref[...] = places
    block_ref[...] = lax.dot_general(
        places, rows_ref[...], (((0,), (0,)), ((), ())), preferred_element_type=F32
    ).astype(BF16)


def text_kernel(scale_ref, shift_ref, block_ref, *refs):
    packets, grad_ref = refs[:STOPS], refs[STOPS]
    scale, shift = scale_ref[0], shift_ref[0]
    text = block_ref[...]
    rows = packets[0].shape[0] - AUX_ROWS
    odd = lax.rem(lax.axis_index("loop"), 2)
    slopes = [
        slopes_for(text, packet[0:rows, :], places_of(packet, stop), scale, shift)
        for stop, packet in zip((0, 2, 1 + 2 * odd, 3 - 2 * odd), packets)
    ]
    for start in range(0, text.shape[1], WIDTH):
        total = None
        for slope, packet in zip(slopes, packets):
            term = jnp.dot(slope, packet[0:rows, start : start + WIDTH], preferred_element_type=F32)
            total = term if total is None else total + term
        grad_ref[:, start : start + WIDTH] = total.astype(BF16)


def send_kernel(places_ref, grad_ref, chunks_hbm, staging, chunks_ref, sent):
    gathered = jnp.dot(places_ref[...], grad_ref[...], preferred_element_type=F32)
    for copy in rows_to_chunks(gathered, staging, chunks_ref, chunks_hbm, sent):
        copy.wait()


def column_copies(source_ref, target_hbm, sent):
    return [
        pltpu.make_async_copy(
            source_ref.at[:, pl.ds(start, WIDTH)], target_hbm.at[:, pl.ds(start, WIDTH)], sent.at[start // WIDTH]
        )
        for start in range(0, source_ref.shape[1], WIDTH)
    ]


def image_kernel(scale_ref, shift_ref, listed_ref, tally_ref, packet_ref, *refs):
    blocks, grad_hbm, owned_ref, grad_ref, sent = refs[:STOPS], *refs[STOPS:]
    owned_ref[...] = owned_rows(listed_ref, tally_ref[0], lax.axis_index("grp"), owned_ref.shape[1])
    scale, shift = scale_ref[0], shift_ref[0]
    rows = grad_ref.shape[0]
    image = packet_ref[0:rows, :]
    odd = lax.rem(lax.axis_index("loop"), 2)
    slopes = [
        slopes_for(block[...], image, places_of(packet_ref, stop), scale, shift)
        for stop, block in zip((0, 2, 3 - 2 * odd, 1 + 2 * odd), blocks)
    ]
    copies = column_copies(grad_ref, grad_hbm, sent)
    for part, copy in enumerate(copies):
        columns = slice(part * WIDTH, (part + 1) * WIDTH)
        total = None
        for slope, block in zip(slopes, blocks):
            term = lax.dot_general(slope, block[:, columns], (((0,), (0,)), ((), ())), preferred_element_type=F32)
            total = term if total is None else total + term
        grad_ref[:, columns] = total
        copy.start()
    for copy in copies:
        copy.wait()


def return_kernel(chunks_ref, owned_ref, grad_hbm, staging, rows_ref, grad_ref, sent):
    chunks_to_rows(chunks_ref, staging, rows_ref)
    owned = owned_ref[...]
    copies = column_copies(grad_ref, grad_hbm, sent)
    for part, copy in enumerate(copies):
        columns = slice(part * WIDTH, (part + 1) * WIDTH)
        grad_ref[:, columns] = lax.dot_general(
            owned, rows_ref[:, columns], (((0,), (0,)), ((), ())), preferred_element_type=F32
        )
        copy.start()
    for copy in copies:
        copy.wait()


def local(
    picture_features,
    caption_features_per_holder,
    dispatched_entries,
    sent_tally,
    positive_caption_position,
    score_scale_factor,
    score_shift_term,
):
    group_count = lax.axis_size("grp")
    loop_count = lax.axis_size("loop")
    image_rows, features = picture_features.shape
    text_rows = caption_features_per_holder.shape[0]
    slot_cap = dispatched_entries.shape[3]
    chunk_rows = slot_cap * features // LANES
    pitch = -(-chunk_rows // 8) * 8

    whole = pl.BlockSpec(memory_space=pltpu.VMEM)
    scalar = pl.BlockSpec(memory_space=pltpu.SMEM)
    remote = pl.BlockSpec(memory_space=pltpu.HBM)
    staging = pltpu.VMEM((group_count * pitch, LANES), F32)
    slot_rows = pltpu.VMEM((group_count * slot_cap, features), BF16)
    chunks = jax.ShapeDtypeStruct((group_count, chunk_rows, LANES), BF16)
    packet_shape = jax.ShapeDtypeStruct((image_rows + AUX_ROWS, features), BF16)
    big = pl.CostEstimate(flops=6 * STOPS * image_rows * text_rows * features, bytes_accessed=8 * image_rows * features, transcendentals=0)
    huge = pl.CostEstimate(flops=50 * 1000 * 1000 * 1000, bytes_accessed=0, transcendentals=0)
    block_shape = jax.ShapeDtypeStruct((text_rows, features), BF16)

    leaving = pltpu.VMEM(chunks.shape, BF16)
    column_sems = pltpu.SemaphoreType.DMA((features // WIDTH,))

    def in_vmem(shape):
        return pltpu.VMEM(shape.shape, shape.dtype)

    def call(kernel, in_specs, out_shape, scratch=(), name=None, cost=None, outs=None):
        return pl.pallas_call(
            kernel,
            out_shape=out_shape,
            in_specs=in_specs,
            out_specs=jax.tree.map(lambda _: whole, out_shape) if outs is None else outs,
            scratch_shapes=list(scratch),
            compiler_params=pltpu.CompilerParams(vmem_limit_bytes=12 * 1024 * 1024),
            name=name,
            cost_estimate=cost,
        )

    def prepare_body(*refs):
        prepare_kernel(loop_count, group_count, *refs)

    def keep_even(*refs):
        relay_kernel(0, *refs)

    def keep_odd(*refs):
        relay_kernel(1, *refs)

    def swapped(value):
        return lax.ppermute(value, "loop", [(source, source ^ 1) for source in range(loop_count)])

    listed = jnp.transpose(dispatched_entries[0], (2, 0, 1))
    packet, outgoing = call(
        prepare_body,
        [remote] * 4,
        (in_vmem(packet_shape), chunks),
        [
            pltpu.VMEM(picture_features.shape, F32),
            pltpu.VMEM((1, image_rows), jnp.int32),
            pltpu.VMEM(caption_features_per_holder.shape, F32),
            pltpu.VMEM(listed.shape, jnp.int32),
            staging,
            leaving,
            pltpu.SemaphoreType.DMA((4,)),
            pltpu.SemaphoreType.DMA((PARTS,)),
        ],
        name="prepare",
        outs=(whole, remote),
    )(
        *[
            pltpu.with_memory_space_constraint(each, pltpu.HBM)
            for each in (
                picture_features,
                positive_caption_position.reshape(1, -1),
                caption_features_per_holder,
                listed,
            )
        ]
    )

    packet_two = passed_along(packet, "loop", -2)
    incoming = lax.all_to_all(outgoing, "grp", split_axis=0, concat_axis=0, tiled=True)
    packet_swap = swapped(packet_two)
    relayed = call(keep_even, [whole] * 2, in_vmem(packet_shape), name="relay_images")(packet, packet_two)
    packet_relay = passed_along(relayed, "loop", -1)

    slot_shape = jax.ShapeDtypeStruct((group_count * slot_cap, text_rows), BF16)
    block, slot_places = call(
        assemble_kernel, [whole] * 2, (in_vmem(block_shape), in_vmem(slot_shape)), [staging, slot_rows], name="assemble"
    )(incoming, sent_tally)

    block_grad = call(text_kernel, [scalar] * 2 + [whole] * (1 + STOPS), in_vmem(block_shape), name="text_grads")(
        score_scale_factor, score_shift_term, block, packet, packet_two, packet_relay, packet_swap
    )
    block_two = pltpu.with_memory_space_constraint(passed_along(block, "loop", 2), pltpu.VMEM)
    sendback = call(
        send_kernel,
        [whole] * 2,
        chunks,
        [staging, leaving, pltpu.SemaphoreType.DMA((PARTS,))],
        name="send_back",
        cost=huge,
        outs=remote,
    )(slot_places, block_grad)
    returned = lax.all_to_all(sendback, "grp", split_axis=0, concat_axis=0, tiled=True)

    relayed_block = call(keep_odd, [whole] * 2, in_vmem(block_shape), name="relay_blocks", cost=huge)(
        block, block_two
    )
    block_relay = passed_along(relayed_block, "loop", 1)
    block_swap = swapped(block_two)
    image_grad, owned = call(
        image_kernel,
        [scalar] * 2 + [whole] * (3 + STOPS),
        (jax.ShapeDtypeStruct((image_rows, features), F32), in_vmem(slot_shape)),
        [pltpu.VMEM((image_rows, features), F32), column_sems],
        name="image_grads",
        cost=big,
        outs=(remote, whole),
    )(score_scale_factor, score_shift_term, listed, sent_tally, packet, block, block_two, block_relay, block_swap)

    text_grad = call(
        return_kernel,
        [whole] * 2,
        jax.ShapeDtypeStruct((text_rows, features), F32),
        [staging, slot_rows, pltpu.VMEM((text_rows, features), F32), column_sems],
        name="give_back",
        outs=remote,
    )(returned, owned)
    return (image_grad, text_grad)


def solution(mesh):
    placed = (
        P(("loop", "grp"), None),
        P(("loop", "grp"), None),
        P("loop", "grp", None, None),
        P("loop", None, None),
        P(("loop", "grp")),
        P(),
        P(),
    )
    return jax.shard_map(
        local,
        mesh=mesh,
        in_specs=placed,
        out_specs=(P(("loop", "grp"), None), P(("loop", "grp"), None)),
        check_vma=False,
    )
```

```python
import jax
import jax.numpy as jnp
from jax import lax
from jax.experimental import pallas as pl
from jax.experimental.pallas import tpu as pltpu
from jax.sharding import PartitionSpec as P

STOPS = 4
LANES = 128
AUX_ROWS = 16
PARTS = 2
WIDTH = 3 * LANES
BF16 = jnp.bfloat16
F32 = jnp.float32


def passed_along(value, axis, steps):
    count = lax.axis_size(axis)
    pairs = [(source, (source + steps) % count) for source in range(count)]
    return lax.ppermute(value, axis, pairs)


def iota(shape, dim):
    return lax.broadcasted_iota(jnp.int32, shape, dim)


def rows_to_chunks(rows, staging, chunks_ref, chunks_hbm, sent):
    peers, chunk_rows, _ = chunks_ref.shape
    pitch = staging.shape[0] // peers
    tiles = rows.shape[1] // LANES
    for slot in range(rows.shape[0] // peers):
        for tile in range(tiles):
            staging[pl.ds(slot * tiles + tile, peers, stride=pitch), :] = rows[
                slot * peers : (slot + 1) * peers, tile * LANES : (tile + 1) * LANES
            ]
    group = peers // PARTS
    copies = []
    for part in range(PARTS):
        for peer in range(part * group, (part + 1) * group):
            chunks_ref[peer] = staging[peer * pitch : peer * pitch + chunk_rows, :].astype(chunks_ref.dtype)
        at = pl.ds(part * group, group)
        copies.append(pltpu.make_async_copy(chunks_ref.at[at], chunks_hbm.at[at], sent.at[part]))
        copies[-1].start()
    return copies


def chunks_to_rows(chunks_ref, staging, rows_ref):
    peers, chunk_rows, _ = chunks_ref.shape
    pitch = staging.shape[0] // peers
    tiles = rows_ref.shape[1] // LANES
    for peer in range(peers):
        staging[peer * pitch : peer * pitch + chunk_rows, :] = chunks_ref[peer].astype(F32)
    for slot in range(rows_ref.shape[0] // peers):
        for tile in range(tiles):
            rows_ref[slot * peers : (slot + 1) * peers, tile * LANES : (tile + 1) * LANES] = staging[
                pl.ds(slot * tiles + tile, peers, stride=pitch), :
            ].astype(rows_ref.dtype)


def hits(columns, width):
    return jnp.concatenate(
        [(column == iota((column.shape[0], width), 1)).astype(F32) for column in columns], axis=0
    ).astype(BF16)


def upright(listed_ref):
    peers = listed_ref.shape[2]
    diagonal = iota((peers, peers), 0) == iota((peers, peers), 1)
    return [
        jnp.sum(jnp.where(diagonal, listed_ref[slot], 0), axis=1, keepdims=True) for slot in range(listed_ref.shape[0])
    ]


def block_places(tally, group_at, slot_cap, width):
    peers = tally.shape[0]
    mine = jnp.where(iota(tally.shape, 1) == group_at, tally, 0)
    before = (iota((peers, peers), 1) < iota((peers, peers), 0)).astype(F32)
    starts = jnp.dot(before, mine.astype(F32), preferred_element_type=F32)
    incoming = jnp.sum(mine, axis=1, keepdims=True)
    first = jnp.sum(starts, axis=1, keepdims=True).astype(jnp.int32)
    return hits([jnp.where(incoming > slot, first + slot, -1) for slot in range(slot_cap)], width)


def places_of(packet_ref, stop):
    rows = packet_ref.shape[0] - AUX_ROWS
    kept = packet_ref[rows:, 0:rows].astype(F32)
    return jnp.sum(jnp.where(iota(kept.shape, 0) == stop, kept, 0.0), axis=0, keepdims=True).astype(jnp.int32)


def owned_rows(listed_ref, tally, group_at, width):
    peers = tally.shape[0]
    mine = jnp.sum(jnp.where(iota(tally.shape, 0) == group_at, tally, 0), axis=0, keepdims=True)
    diagonal = iota((peers, peers), 0) == iota((peers, peers), 1)
    outgoing = jnp.sum(jnp.where(diagonal, mine, 0), axis=1, keepdims=True)
    return hits([jnp.where(outgoing > slot, rows, -1) for slot, rows in enumerate(upright(listed_ref))], width)


def slopes_for(text, image, places, scale, shift):
    scores = lax.dot_general(text, image, (((1,), (1,)), ((), ())), preferred_element_type=F32)
    logits = scale * scores + shift
    positive = places == iota(scores.shape, 0)
    toward = jax.nn.sigmoid(jnp.where(positive, -logits, logits))
    return (jnp.where(positive, -scale, scale) * toward).astype(BF16)


def prepare_kernel(
    loop_count,
    group_count,
    picture_hbm,
    positive_hbm,
    caption_hbm,
    listed_hbm,
    packet_ref,
    chunks_hbm,
    picture_ref,
    positive_ref,
    caption_ref,
    listed_ref,
    staging,
    chunks_ref,
    arrived,
    sent,
):
    copies = [
        pltpu.make_async_copy(source, target, arrived.at[at])
        for at, (source, target) in enumerate(
            [
                (listed_hbm, listed_ref),
                (caption_hbm, caption_ref),
                (positive_hbm, positive_ref),
                (picture_hbm, picture_ref),
            ]
        )
    ]
    for copy in copies:
        copy.start()
    text_rows = caption_ref.shape[0]
    copies[0].wait()
    chosen = hits(upright(listed_ref), text_rows)
    copies[1].wait()
    gathered = jnp.dot(chosen, caption_ref[...].astype(BF16), preferred_element_type=F32)
    leaving = rows_to_chunks(gathered, staging, chunks_ref, chunks_hbm, sent)
    rows = picture_ref.shape[0]
    copies[2].wait()
    positive = positive_ref[...]
    anchor = positive // (group_count * text_rows)
    behind = lax.rem(lax.axis_index("loop") - anchor + loop_count, loop_count)
    place = lax.rem(positive, text_rows)
    packet_ref[rows:, :] = jnp.zeros((AUX_ROWS, packet_ref.shape[1]), BF16)
    packet_ref[rows:, 0:rows] = jnp.where(behind == iota((AUX_ROWS, rows), 0), place, -1).astype(F32).astype(BF16)
    copies[3].wait()
    packet_ref[0:rows, :] = picture_ref[...].astype(BF16)
    for copy in leaving:
        copy.wait()


def relay_kernel(passing, own_ref, arrived_ref, out_ref):
    parity = lax.rem(lax.axis_index("loop"), 2)

    @pl.when(parity == passing)
    def _():
        out_ref[...] = arrived_ref[...]

    @pl.when(parity != passing)
    def _():
        out_ref[...] = own_ref[...]


def assemble_kernel(chunks_ref, tally_ref, block_ref, places_ref, staging, rows_ref):
    slot_cap = rows_ref.shape[0] // chunks_ref.shape[0]
    chunks_to_rows(chunks_ref, staging, rows_ref)
    places = block_places(tally_ref[0], lax.axis_index("grp"), slot_cap, block_ref.shape[0])
    places_ref[...] = places
    block_ref[...] = lax.dot_general(
        places, rows_ref[...], (((0,), (0,)), ((), ())), preferred_element_type=F32
    ).astype(BF16)


def text_kernel(scale_ref, shift_ref, block_ref, *refs):
    packets, grad_ref = refs[:STOPS], refs[STOPS]
    scale, shift = scale_ref[0], shift_ref[0]
    text = block_ref[...]
    rows = packets[0].shape[0] - AUX_ROWS
    odd = lax.rem(lax.axis_index("loop"), 2)
    slopes = [
        slopes_for(text, packet[0:rows, :], places_of(packet, stop), scale, shift)
        for stop, packet in zip((0, 2, 1 + 2 * odd, 3 - 2 * odd), packets)
    ]
    for start in range(0, text.shape[1], WIDTH):
        total = None
        for slope, packet in zip(slopes, packets):
            term = jnp.dot(slope, packet[0:rows, start : start + WIDTH], preferred_element_type=F32)
            total = term if total is None else total + term
        grad_ref[:, start : start + WIDTH] = total.astype(BF16)


def send_kernel(places_ref, grad_ref, chunks_hbm, staging, chunks_ref, sent):
    gathered = jnp.dot(places_ref[...], grad_ref[...], preferred_element_type=F32)
    for copy in rows_to_chunks(gathered, staging, chunks_ref, chunks_hbm, sent):
        copy.wait()


def column_copies(source_ref, target_hbm, sent):
    return [
        pltpu.make_async_copy(
            source_ref.at[:, pl.ds(start, WIDTH)], target_hbm.at[:, pl.ds(start, WIDTH)], sent.at[start // WIDTH]
        )
        for start in range(0, source_ref.shape[1], WIDTH)
    ]


def image_kernel(scale_ref, shift_ref, listed_ref, tally_ref, packet_ref, *refs):
    blocks, grad_hbm, owned_ref, grad_ref, sent = refs[:STOPS], *refs[STOPS:]
    owned_ref[...] = owned_rows(listed_ref, tally_ref[0], lax.axis_index("grp"), owned_ref.shape[1])
    scale, shift = scale_ref[0], shift_ref[0]
    rows = grad_ref.shape[0]
    image = packet_ref[0:rows, :]
    odd = lax.rem(lax.axis_index("loop"), 2)
    slopes = [
        slopes_for(block[...], image, places_of(packet_ref, stop), scale, shift)
        for stop, block in zip((0, 2, 3 - 2 * odd, 1 + 2 * odd), blocks)
    ]
    copies = column_copies(grad_ref, grad_hbm, sent)
    for part, copy in enumerate(copies):
        columns = slice(part * WIDTH, (part + 1) * WIDTH)
        total = None
        for slope, block in zip(slopes, blocks):
            term = lax.dot_general(slope, block[:, columns], (((0,), (0,)), ((), ())), preferred_element_type=F32)
            total = term if total is None else total + term
        grad_ref[:, columns] = total
        copy.start()
    for copy in copies:
        copy.wait()


def return_kernel(chunks_ref, owned_ref, grad_hbm, staging, rows_ref, grad_ref, sent):
    chunks_to_rows(chunks_ref, staging, rows_ref)
    owned = owned_ref[...]
    copies = column_copies(grad_ref, grad_hbm, sent)
    for part, copy in enumerate(copies):
        columns = slice(part * WIDTH, (part + 1) * WIDTH)
        grad_ref[:, columns] = lax.dot_general(
            owned, rows_ref[:, columns], (((0,), (0,)), ((), ())), preferred_element_type=F32
        )
        copy.start()
    for copy in copies:
        copy.wait()


def local(
    picture_features,
    caption_features_per_holder,
    dispatched_entries,
    sent_tally,
    positive_caption_position,
    score_scale_factor,
    score_shift_term,
):
    group_count = lax.axis_size("grp")
    loop_count = lax.axis_size("loop")
    image_rows, features = picture_features.shape
    text_rows = caption_features_per_holder.shape[0]
    slot_cap = dispatched_entries.shape[3]
    chunk_rows = slot_cap * features // LANES
    pitch = -(-chunk_rows // 8) * 8

    whole = pl.BlockSpec(memory_space=pltpu.VMEM)
    scalar = pl.BlockSpec(memory_space=pltpu.SMEM)
    remote = pl.BlockSpec(memory_space=pltpu.HBM)
    staging = pltpu.VMEM((group_count * pitch, LANES), F32)
    slot_rows = pltpu.VMEM((group_count * slot_cap, features), BF16)
    chunks = jax.ShapeDtypeStruct((group_count, chunk_rows, LANES), BF16)
    packet_shape = jax.ShapeDtypeStruct((image_rows + AUX_ROWS, features), BF16)
    big = pl.CostEstimate(flops=6 * STOPS * image_rows * text_rows * features, bytes_accessed=8 * image_rows * features, transcendentals=0)
    huge = pl.CostEstimate(flops=50 * 1000 * 1000 * 1000, bytes_accessed=0, transcendentals=0)
    block_shape = jax.ShapeDtypeStruct((text_rows, features), BF16)

    leaving = pltpu.VMEM(chunks.shape, BF16)
    column_sems = pltpu.SemaphoreType.DMA((features // WIDTH,))

    def in_vmem(shape):
        return pltpu.VMEM(shape.shape, shape.dtype)

    def call(kernel, in_specs, out_shape, scratch=(), name=None, cost=None, outs=None):
        return pl.pallas_call(
            kernel,
            out_shape=out_shape,
            in_specs=in_specs,
            out_specs=jax.tree.map(lambda _: whole, out_shape) if outs is None else outs,
            scratch_shapes=list(scratch),
            compiler_params=pltpu.CompilerParams(vmem_limit_bytes=12 * 1024 * 1024),
            name=name,
            cost_estimate=cost,
        )

    def prepare_body(*refs):
        prepare_kernel(loop_count, group_count, *refs)

    def keep_even(*refs):
        relay_kernel(0, *refs)

    def keep_odd(*refs):
        relay_kernel(1, *refs)

    def swapped(value):
        return lax.ppermute(value, "loop", [(source, source ^ 1) for source in range(loop_count)])

    listed = jnp.transpose(dispatched_entries[0], (2, 0, 1))
    packet, outgoing = call(
        prepare_body,
        [remote] * 4,
        (in_vmem(packet_shape), chunks),
        [
            pltpu.VMEM(picture_features.shape, F32),
            pltpu.VMEM((1, image_rows), jnp.int32),
            pltpu.VMEM(caption_features_per_holder.shape, F32),
            pltpu.VMEM(listed.shape, jnp.int32),
            staging,
            leaving,
            pltpu.SemaphoreType.DMA((4,)),
            pltpu.SemaphoreType.DMA((PARTS,)),
        ],
        name="prepare",
        outs=(whole, remote),
    )(
        *[
            pltpu.with_memory_space_constraint(each, pltpu.HBM)
            for each in (
                picture_features,
                positive_caption_position.reshape(1, -1),
                caption_features_per_holder,
                listed,
            )
        ]
    )

    packet_two = passed_along(packet, "loop", -2)
    incoming = lax.all_to_all(outgoing, "grp", split_axis=0, concat_axis=0, tiled=True)
    packet_swap = swapped(packet_two)
    relayed = call(keep_even, [whole] * 2, in_vmem(packet_shape), name="relay_images")(packet, packet_two)
    packet_relay = passed_along(relayed, "loop", -1)

    slot_shape = jax.ShapeDtypeStruct((group_count * slot_cap, text_rows), BF16)
    block, slot_places = call(
        assemble_kernel, [whole] * 2, (in_vmem(block_shape), in_vmem(slot_shape)), [staging, slot_rows], name="assemble"
    )(incoming, sent_tally)

    block_grad = call(text_kernel, [scalar] * 2 + [whole] * (1 + STOPS), in_vmem(block_shape), name="text_grads")(
        score_scale_factor, score_shift_term, block, packet, packet_two, packet_relay, packet_swap
    )
    block_two = pltpu.with_memory_space_constraint(passed_along(block, "loop", 2), pltpu.VMEM)
    sendback = call(
        send_kernel,
        [whole] * 2,
        chunks,
        [staging, leaving, pltpu.SemaphoreType.DMA((PARTS,))],
        name="send_back",
        cost=huge,
        outs=remote,
    )(slot_places, block_grad)
    returned = lax.all_to_all(sendback, "grp", split_axis=0, concat_axis=0, tiled=True)

    relayed_block = call(keep_odd, [whole] * 2, in_vmem(block_shape), name="relay_blocks", cost=huge)(
        block, block_two
    )
    block_relay = passed_along(relayed_block, "loop", 1)
    block_swap = swapped(block_two)
    image_grad, owned = call(
        image_kernel,
        [scalar] * 2 + [whole] * (3 + STOPS),
        (jax.ShapeDtypeStruct((image_rows, features), F32), in_vmem(slot_shape)),
        [pltpu.VMEM((image_rows, features), F32), column_sems],
        name="image_grads",
        cost=big,
        outs=(remote, whole),
    )(score_scale_factor, score_shift_term, listed, sent_tally, packet, block, block_two, block_relay, block_swap)

    text_grad = call(
        return_kernel,
        [whole] * 2,
        jax.ShapeDtypeStruct((text_rows, features), F32),
        [staging, slot_rows, pltpu.VMEM((text_rows, features), F32), column_sems],
        name="give_back",
        outs=remote,
    )(returned, owned)
    return (image_grad, text_grad)


def solution(mesh):
    placed = (
        P(("loop", "grp"), None),
        P(("loop", "grp"), None),
        P("loop", "grp", None, None),
        P("loop", None, None),
        P(("loop", "grp")),
        P(),
        P(),
    )
    return jax.shard_map(
        local,
        mesh=mesh,
        in_specs=placed,
        out_specs=(P(("loop", "grp"), None), P(("loop", "grp"), None)),
        check_vma=False,
    )
```
